128 devices in a mesh: theta: 16 (over z, x), phi: 8 (over y, core).
Axes of the slice: x: 4, y: 4, z: 4, core: 2. Of those that a mesh axis runs over, the one named last changes fastest.
Arguments:
- alm: bfloat16 [512, 2, 8192], P(('theta', 'phi')), may hold values from -6 to 6
- wig: bfloat16 [512, 256, 8192], P(('theta', 'phi')), may hold values from -0.0625 to 0.0625
- slot_order: int32 [512], replicated, may hold values from 0 to 511, each once
- beam: bfloat16 [8192, 128], replicated, may hold values from -6 to 6
- phi_cell: int32 [524288], P(('theta', 'phi')), may hold values from 0 to 192
- theta_cell: int32 [524288], P(('theta', 'phi')), may hold values from 0 to 16
- orient_cell_index: int32 [524288], P(('theta', 'phi')), may hold values from 0 to 127
- tap_weight: float32 [8, 524288], P(None, ('theta', 'phi')), may hold values from 0 to 1
- sample_count: int32 [128], P(('theta', 'phi')), may hold values from 1638 to 4096, as said below
Outputs:
- samples_out: float32 [524288], P(('theta', 'phi'))
The draws below stay inside these ranges and needn't reach their ends.
Inputs may be any that keep to these rules, and one draw needn't show every extreme that they name: `sample_count`: entry g counts the live samples of device g, which are its first slots; some device has exactly 4096.
All inputs are finite; a program needn't handle non-finite values.
Results may differ from the reference program's by a relative error of at most 0.0062.
Values may be sent and summed in bfloat16 or wider, within the bound.
A program may use at most 192 MiB of HBM per device.

```python
import math
import jax
import jax.numpy as jnp
from jax import lax

LDEG = 8192
K = 128
PSI = 128
RT = 16
PD = 192
S_CAP = 4096
M_ALL = 512
CYCLES = 256
PHI_ALL = 1536
SAMPLES = 524288
N_PHI = 8
DEVICES = 128


def draw_sample_count(key, part):
    key = jax.random.fold_in(key, 11)
    first, right_factor = jax.random.split(key)
    counts = jax.random.randint(first, (DEVICES,), 2 * S_CAP // 5, S_CAP + 1)
    fullest = jax.random.randint(right_factor, (), 0, DEVICES)
    return jnp.where(jnp.arange(DEVICES) == fullest, S_CAP, counts).astype(jnp.int32)


def place_ends(values, key, least, top_value):
    index_at = [jax.random.randint(jax.random.fold_in(key, axis), (), 0, length) for axis, length in enumerate(values.shape)]
    widest = values.shape.index(max(values.shape))
    beside = index_at[:widest] + [(index_at[widest] + 1) % values.shape[widest]] + index_at[widest + 1:]
    return values.at[tuple(index_at)].set(least).at[tuple(beside)].set(top_value)


def block_levels(key, shape, shards, low, top_value):
    factor_of, own = 1.0, jax.random.fold_in(key, 6)
    for axis_at, shards_of in shards:
        heights = jnp.exp(jax.random.uniform(jax.random.fold_in(own, axis_at), (shards_of,), jnp.float32, low / len(shards), top_value / len(shards)))
        factor_of = factor_of * jnp.repeat(heights, shape[axis_at] // shards_of).reshape([-1 if axis == axis_at else 1 for axis in range(len(shape))])
    return factor_of


def gaussian(stream_key, dims, spread, bound, cuts=(), held_as=jnp.bfloat16):
    loudness = block_levels(stream_key, dims, cuts, -0.22, 0.18) if cuts else 1.0
    drawn = jax.random.normal(stream_key, dims, jnp.float32) * spread * loudness
    return jnp.minimum(jnp.maximum(drawn, -bound), bound).astype(held_as)


def setup_inputs(seed: int = 0) -> dict:
    key_list = jax.random.split(jax.random.key(seed), 10)
    return {
        "alm": gaussian(key_list[0], (M_ALL, 2, LDEG), 1.0, 6.0, ((0, 128),)),
        "wig": gaussian(key_list[1], (M_ALL, CYCLES, LDEG), LDEG ** -0.5, 0.0625, ((0, 128),)),
        "slot_order": jax.random.permutation(key_list[2], M_ALL).astype(jnp.int32),
        "beam": gaussian(key_list[3], (LDEG, K), 1.0, 6.0),
        "phi_cell": place_ends(jax.random.randint(key_list[4], (SAMPLES,), 0, PD + 1), jax.random.fold_in(key_list[4], 1), 0, PD).astype(jnp.int32),
        "theta_cell": place_ends(jax.random.randint(key_list[5], (SAMPLES,), 0, RT + 1), jax.random.fold_in(key_list[5], 1), 0, RT).astype(jnp.int32),
        "orient_cell_index": place_ends(jax.random.randint(key_list[6], (SAMPLES,), 0, PSI), jax.random.fold_in(key_list[6], 1), 0, PSI - 1).astype(jnp.int32),
        "tap_weight": jnp.clip(1.0 * jax.random.uniform(key_list[7], (8, SAMPLES), jnp.float32) ** block_levels(key_list[7], (8, SAMPLES), ((1, 128),), -0.2, 0.2), 0.0, 1.0),
        "sample_count": draw_sample_count(jax.random.fold_in(key_list[9], 71), 0),
    }


def slot_m_values(slot_order, half_phi, m_all):
    stride = max(half_phi // m_all, 1)
    return slot_order * half_phi // m_all + 7 * slot_order % stride

def weighted_sky(alm_rows, beam, m_value):
    degree = jnp.arange(alm_rows.shape[1], dtype=jnp.int32)
    sky = jnp.where(degree[None, :] >= m_value, alm_rows.astype(jnp.float32), jnp.float32(0.0))
    factor_product = sky.T[:, :, None] * beam.astype(jnp.float32)[:, None, :]
    return factor_product.reshape(factor_product.shape[0], -1).astype(jnp.bfloat16)

def cycle_orders(alm_rows, wigner_rows, beam, m_value):
    left_factor = weighted_sky(alm_rows, beam, m_value)
    return jnp.dot(wigner_rows, left_factor, preferred_element_type=jnp.float32).astype(jnp.bfloat16)

def phi_table(m_values, phi_index, total_phi, count_m):
    phase = m_values[:, None] * phi_index[None, :] % total_phi
    angle = phase.astype(jnp.float32) * (2.0 * math.pi / total_phi)
    scale = 1.0 / math.sqrt(count_m)
    cosine = jnp.cos(angle) * scale
    sine = jnp.sin(angle) * scale
    table = jnp.stack([jnp.stack([cosine, sine], -1), jnp.stack([-sine, cosine], -1)], 1)
    return table.astype(jnp.bfloat16)

def psi_table(order_count, psi_count):
    orders = jnp.arange(order_count, dtype=jnp.int32)
    points = jnp.arange(psi_count, dtype=jnp.int32)
    phase = orders[:, None] * points[None, :] % psi_count
    angle = phase.astype(jnp.float32) * (2.0 * math.pi / psi_count)
    scale = 1.0 / math.sqrt(2 * order_count)
    return jnp.stack([jnp.cos(angle) * scale, -jnp.sin(angle) * scale], 0).astype(jnp.bfloat16)

def interpolate(flat, phi_base, theta_base, orient_cell_index, tap_weight, width, psi_count):
    total = jnp.zeros(phi_base.shape, jnp.float32)
    for tap_phi in range(2):
        for tap_theta in range(2):
            for tap_psi in range(2):
                place = ((phi_base + tap_phi) * width + theta_base + tap_theta) * psi_count + (orient_cell_index + tap_psi) % psi_count
                total = total + tap_weight[4 * tap_phi + 2 * tap_theta + tap_psi] * jnp.take(flat, place)
    return total

def reference(alm, wig, slot_order, beam, phi_cell, theta_cell, orient_cell_index, tap_weight, sample_count):
    m_values = slot_m_values(slot_order, PHI_ALL // 2, M_ALL)
    orders = lax.map(lambda item: cycle_orders(item[0], item[1], beam, item[2]), (alm, wig, m_values))
    rows = orders.reshape(M_ALL, CYCLES, 2, K)
    table = phi_table(m_values, jnp.arange(PHI_ALL, dtype=jnp.int32), PHI_ALL, M_ALL)
    spectrum = jnp.einsum('ncqd,ntck->qtdk', table.astype(jnp.float32), rows.astype(jnp.float32)).astype(jnp.bfloat16)
    cube = jnp.einsum('qtdk,dkp->qtp', spectrum.astype(jnp.float32), psi_table(K, PSI).astype(jnp.float32))
    padded = jnp.pad(cube, ((0, 0), (1, 1), (0, 0)))
    padded = jnp.concatenate([padded[-1:], padded, padded[:1]], 0)
    flat = padded.reshape(-1)
    device = jnp.arange(SAMPLES, dtype=jnp.int32) // S_CAP
    phi_base = device % N_PHI * PD + phi_cell
    theta_base = device // N_PHI * RT + theta_cell
    value = interpolate(flat, phi_base, theta_base, orient_cell_index, tap_weight, CYCLES + 2, PSI)
    live = jnp.arange(SAMPLES, dtype=jnp.int32) % S_CAP < sample_count[device]
    return jnp.where(live, value, jnp.float32(0.0))
```

```python
import functools
import math

import jax
import jax.numpy as jnp
from jax import lax
from jax.experimental import pallas as pl
from jax.experimental.pallas import tpu as pltpu
from jax.sharding import PartitionSpec as P

PSI = 128
PD = 192
QP = 200
CH = 4
MESH = pl.DeviceIdType.MESH
ORDER = (0, 3, 1, 2)


def slot_m(order, half, m_all):
    stride = max(half // m_all, 1)
    m = lax.shift_right_logical(order * half, m_all.bit_length() - 1)
    if stride > 1:
        m = m + (7 * order) % stride
    return m


def turn_cos(phase, total):
    x = (jnp.abs(phase - total / 2) - total / 4) * (2.0 * math.pi / total)
    x2 = x * x
    p = jnp.float32(-1.0 / math.factorial(11))
    for n in (9, 7, 5, 3, 1):
        p = p * x2 + jnp.float32((-1) ** (n // 2) / math.factorial(n))
    return p * x


def wrap(value, total):
    return value - jnp.floor((value + 0.5) * jnp.float32(1.0 / total)) * total


def orders_kernel(
    n_theta, n_phi, slots, ldeg, tile, m_all,
    wig_hbm, alm_ref, beam_hbm, order_ref, order_smem, cube_ref,
    wig_v, beam_v, beam_t, x32, x16, landed, grid_v, table_v, halo_v,
    wig_sem, beam_sem, a_send, a_recv, y_send, y_recv, f_send, f_recv, s_send, s_recv, h_send, h_recv,
):
    me_t = lax.axis_index("theta")
    me_p = lax.axis_index("phi")
    me_y, me_c = me_p // 2, me_p % 2
    n_y = n_phi // 2
    total = PD * n_phi
    rt = 4 * CH
    rows = rt * 8 // CH
    per = rt // CH
    tiles = ldeg // tile

    def at(t, y, c):
        return (t, y * 2 + c)

    y_up, y_down, y_far = (me_y + 1) % n_y, (me_y + n_y - 1) % n_y, (me_y + 2) % n_y
    own = me_p
    block = {"own": own, "down": y_down * 2 + me_c, "up": y_up * 2 + me_c, "far": y_far * 2 + me_c}

    beam_copy = pltpu.make_async_copy(beam_hbm, beam_v, beam_sem)
    beam_copy.start()

    def wig_copy(s, i):
        span = pl.ds(i * tile, tile)
        return pltpu.make_async_copy(wig_hbm.at[s, :, span], wig_v.at[s, :, span], wig_sem.at[s, i])

    for s in range(slots):
        for i in range(tiles):
            wig_copy(s, i).start()

    barrier = pltpu.get_barrier_semaphore()

    def greet(k, _):
        pl.semaphore_signal(
            barrier, inc=1, device_id=at(lax.rem(me_t + k, n_theta), me_y, me_c), device_id_type=MESH
        )
        return 0

    lax.fori_loop(1, n_theta, greet, 0)
    for y, c in ((y_up, me_c), (y_down, me_c), (me_y, 1 - me_c)):
        pl.semaphore_signal(barrier, inc=1, device_id=at(me_t, y, c), device_id_type=MESH)

    eye = (
        lax.broadcasted_iota(jnp.int32, (128, 128), 0) == lax.broadcasted_iota(jnp.int32, (128, 128), 1)
    ).astype(jnp.bfloat16)
    beam_copy.wait()
    for i in range(tiles):
        beam_t[:, i * tile:(i + 1) * tile] = lax.dot_general(
            eye, beam_v[i * tile:(i + 1) * tile, :], (((1,), (1,)), ((), ())),
            preferred_element_type=jnp.float32,
        ).astype(jnp.bfloat16)

    k_at = lax.broadcasted_iota(jnp.int32, (128, 128), 0)
    p_at = lax.broadcasted_iota(jnp.int32, (128, 128), 1)
    turn = ((k_at * p_at) % PSI).astype(jnp.float32)
    scale = 1.0 / math.sqrt(2 * 128)
    psi0 = (turn_cos(turn, PSI) * scale).astype(jnp.bfloat16)
    psi1 = (-turn_cos(wrap(turn - PSI / 4 + PSI, PSI), PSI) * scale).astype(jnp.bfloat16)
    psi = jnp.concatenate(
        [jnp.concatenate([psi0, psi1], axis=1), jnp.concatenate([psi1, -psi0], axis=1)], axis=0
    )

    for s in range(slots):
        m_own = slot_m(order_smem[(me_t * n_phi + me_p) * slots + s], total // 2, m_all)
        acc = None
        for i in range(tiles):
            degree = lax.broadcasted_iota(jnp.int32, (2, tile), 1) + i * tile
            sky = jnp.where(
                degree >= m_own, alm_ref[s, :, i * tile:(i + 1) * tile].astype(jnp.float32), 0.0
            )
            part = beam_t[:, i * tile:(i + 1) * tile]
            weighted = jnp.concatenate(
                [
                    part * jnp.broadcast_to(sky[c:c + 1, :], (128, tile)).astype(jnp.bfloat16)
                    for c in range(2)
                ],
                axis=0,
            )
            wig_copy(s, i).wait()
            term = lax.dot_general(
                weighted, wig_v[s, :, i * tile:(i + 1) * tile], (((1,), (1,)), ((), ())),
                preferred_element_type=jnp.float32,
            )
            acc = term if acc is None else acc + term
        x = lax.dot_general(
            acc.astype(jnp.bfloat16), psi, (((0,), (0,)), ((), ())), preferred_element_type=jnp.float32
        )
        for c in range(2):
            x32[pl.ds(2 * s + c, n_theta * rt, stride=8), :] = x[:, c * 128:(c + 1) * 128]

    x16[...] = x32[...].astype(jnp.bfloat16)
    pl.semaphore_wait(barrier, n_theta + 2)

    for j in ORDER:
        def send(k, _):
            t = lax.rem(me_t + k, n_theta)
            src = x16.at[pl.ds(pl.multiple_of(t * rt * 8 + j * rows, 16), rows), :]
            pltpu.make_async_remote_copy(
                src_ref=src, dst_ref=landed.at[j, me_t], send_sem=a_send.at[j], recv_sem=a_recv.at[j],
                device_id=at(t, me_y, me_c), device_id_type=MESH,
            ).start()
            return 0

        lax.fori_loop(1, n_theta, send, 0)
        landed[j, me_t] = x16[pl.ds(pl.multiple_of(me_t * rt * 8 + j * rows, 16), rows), :]

    k_all = n_phi * n_theta * 2 * slots
    so = order_ref[...]
    m_row = slot_m(so, total // 2, m_all)
    m_hi = lax.shift_right_logical(m_row, 4).astype(jnp.float32)
    m_lo = (m_row & 15).astype(jnp.float32)
    both = jnp.concatenate([m_hi, m_lo, jnp.zeros((6, m_all), jnp.float32)], axis=0).astype(jnp.bfloat16)
    n_at = lax.broadcasted_iota(jnp.int32, (m_all, k_all), 0)
    col = lax.broadcasted_iota(jnp.int32, (m_all, k_all), 1)
    per_block = n_theta * 2 * slots
    slot_at = (col % per_block // (2 * slots) * n_phi + col // per_block) * slots + col % (2 * slots) // 2
    pick = (n_at == slot_at).astype(jnp.bfloat16)
    moved = jnp.dot(both, pick, preferred_element_type=jnp.float32)
    m_col = moved[0:1, :] * 16.0 + moved[1:2, :]
    q_at = lax.broadcasted_iota(jnp.int32, (QP, k_all), 0) + (me_p * PD - 1 + total)
    part_at = (lax.broadcasted_iota(jnp.int32, (1, k_all), 1) % 2).astype(jnp.float32)
    phase = wrap(m_col * q_at.astype(jnp.float32) + (1.0 - part_at * 0.25) * total, total)
    table_v[...] = (turn_cos(phase, total) * (1.0 / math.sqrt(m_all))).astype(jnp.bfloat16)

    def share(j, which, n):
        b = block[which]
        return pltpu.make_async_remote_copy(
            src_ref=grid_v.at[j, b], dst_ref=grid_v.at[j, b], send_sem=s_send.at[j, n], recv_sem=s_recv.at[j, n],
            device_id=at(me_t, me_y, 1 - me_c), device_id_type=MESH,
        )

    def pass_y(j, n, up):
        return pltpu.make_async_remote_copy(
            src_ref=grid_v.at[j, own], dst_ref=grid_v.at[j, own], send_sem=y_send.at[j, n],
            recv_sem=y_recv.at[j, n], device_id=at(me_t, y_up if up else y_down, me_c), device_id_type=MESH,
        )

    def forward(j, n, up):
        half = pl.ds(n * (per // 2), per // 2)
        b = block["down" if up else "up"]
        return pltpu.make_async_remote_copy(
            src_ref=grid_v.at[j, b, half], dst_ref=grid_v.at[j, b, half], send_sem=f_send.at[j, n],
            recv_sem=f_recv.at[j, n], device_id=at(me_t, y_up if up else y_down, me_c), device_id_type=MESH,
        )

    for j in ORDER:
        pltpu.make_async_remote_copy(
            src_ref=landed.at[j, pl.ds(0, n_theta - 1)], dst_ref=landed.at[j, pl.ds(0, n_theta - 1)],
            send_sem=a_send.at[j], recv_sem=a_recv.at[j], device_id=at(me_t, me_y, me_c), device_id_type=MESH,
        ).wait_recv()
        for pair in range(per // 2):
            both_r = landed[j, :, pair * 16:(pair + 1) * 16, :].astype(jnp.float32)
            for n in range(2):
                grid_v[j, own, 2 * pair + n] = (
                    both_r[:, n * 8:(n + 1) * 8, :].reshape(n_theta * 8, 128).astype(jnp.bfloat16)
                )
        pass_y(j, 0, True).start()
        pass_y(j, 1, False).start()
        share(j, "own", 0).start()

    for j in ORDER:
        pass_y(j, 0, True).wait_recv()
        forward(j, 0, True).start()
        share(j, "down", 1).start()
        pass_y(j, 1, False).wait_recv()
        forward(j, 1, False).start()
        share(j, "up", 2).start()

    def halo(n, row):
        t = me_t + 1 if n == 0 else me_t - 1
        return pltpu.make_async_remote_copy(
            src_ref=cube_ref.at[row], dst_ref=halo_v.at[n], send_sem=h_send.at[n], recv_sem=h_recv.at[n],
            device_id=at(lax.rem(t + n_theta, n_theta), me_y, me_c), device_id_type=MESH,
        )

    for j in ORDER:
        forward(j, 0, True).wait_recv()
        forward(j, 1, False).wait_recv()
        share(j, "far", 3).start()
        for n, which in enumerate(("own", "down", "up", "far")):
            share(j, which, n).wait_recv()
        for pair in range(per // 2):
            right = jnp.concatenate(
                [grid_v[j, :, 2 * pair + n].reshape(k_all, 128) for n in range(2)], axis=1
            )
            tile_out = jnp.dot(table_v[...], right, preferred_element_type=jnp.float32)
            for n in range(2):
                cube_ref[1 + j * per + 2 * pair + n] = tile_out[:, n * 128:(n + 1) * 128]
        if j == CH - 1:
            @pl.when(me_t < n_theta - 1)
            def _():
                halo(0, rt).start()
        if j == 0:
            @pl.when(me_t > 0)
            def _():
                halo(1, 1).start()

    @pl.when(me_t > 0)
    def _():
        halo(0, rt).wait_recv()
        cube_ref[0] = halo_v[0]

    @pl.when(me_t == 0)
    def _():
        cube_ref[0] = jnp.zeros((QP, 128), jnp.float32)

    @pl.when(me_t < n_theta - 1)
    def _():
        halo(1, 1).wait_recv()
        cube_ref[rt + 1] = halo_v[1]
        halo(0, rt).wait_send()

    @pl.when(me_t == n_theta - 1)
    def _():
        cube_ref[rt + 1] = jnp.zeros((QP, 128), jnp.float32)

    @pl.when(me_t > 0)
    def _():
        halo(1, 1).wait_send()

    for j in ORDER:
        pltpu.make_async_remote_copy(
            src_ref=landed.at[j, pl.ds(0, n_theta - 1)], dst_ref=landed.at[j, pl.ds(0, n_theta - 1)],
            send_sem=a_send.at[j], recv_sem=a_recv.at[j], device_id=at(me_t, me_y, me_c), device_id_type=MESH,
        ).wait_send()
        pass_y(j, 0, True).wait_send()
        pass_y(j, 1, False).wait_send()
        forward(j, 0, True).wait_send()
        forward(j, 1, False).wait_send()
        for n, which in enumerate(("own", "down", "up", "far")):
            share(j, which, n).wait_send()


def make_cube(alm, wig, slot_order, beam):
    n_theta, n_phi = lax.axis_size("theta"), lax.axis_size("phi")
    slots, _, ldeg = alm.shape
    m_all = slot_order.shape[0]
    rt = 4 * CH
    per = rt // CH
    tile = min(ldeg, 2048)
    vmem = pl.BlockSpec(memory_space=pltpu.VMEM)
    anywhere = pl.BlockSpec(memory_space=pl.ANY)
    k_all = n_phi * n_theta * 2 * slots
    return pl.pallas_call(
        functools.partial(orders_kernel, n_theta, n_phi, slots, ldeg, tile, m_all),
        out_shape=jax.ShapeDtypeStruct((rt + 2, QP, 128), jnp.float32),
        in_specs=[anywhere, vmem, anywhere, vmem, pl.BlockSpec(memory_space=pltpu.SMEM)],
        out_specs=vmem,
        scratch_shapes=[
            pltpu.VMEM(wig.shape, jnp.bfloat16),
            pltpu.VMEM(beam.shape, jnp.bfloat16),
            pltpu.VMEM(beam.shape[::-1], jnp.bfloat16),
            pltpu.VMEM((n_theta * rt * 8, 128), jnp.float32),
            pltpu.VMEM((n_theta * rt * 8, 128), jnp.bfloat16),
            pltpu.VMEM((CH, n_theta, per * 8, 128), jnp.bfloat16),
            pltpu.VMEM((CH, n_phi, per, n_theta * 8, 128), jnp.bfloat16),
            pltpu.VMEM((QP, k_all), jnp.bfloat16),
            pltpu.VMEM((2, QP, 128), jnp.float32),
            pltpu.SemaphoreType.DMA((slots, ldeg // tile)),
            pltpu.SemaphoreType.DMA,
            pltpu.SemaphoreType.DMA((CH,)),
            pltpu.SemaphoreType.DMA((CH,)),
            pltpu.SemaphoreType.DMA((CH, 2)),
            pltpu.SemaphoreType.DMA((CH, 2)),
            pltpu.SemaphoreType.DMA((CH, 2)),
            pltpu.SemaphoreType.DMA((CH, 2)),
            pltpu.SemaphoreType.DMA((CH, 4)),
            pltpu.SemaphoreType.DMA((CH, 4)),
            pltpu.SemaphoreType.DMA((2,)),
            pltpu.SemaphoreType.DMA((2,)),
        ],
        compiler_params=pltpu.CompilerParams(
            collective_id=0, has_side_effects=True, vmem_limit_bytes=56 << 20
        ),
        name="make_cube",
    )(wig, alm, beam, slot_order.reshape(1, -1), slot_order)


def sample_kernel(cells, base_ref, shift_ref, count_ref, cube_ref, weight_ref, out_ref, taps):
    def build(r, _):
        first = cube_ref[r]
        for e, rows in ((0, first), (1, pltpu.roll(first, PSI - 1, 1))):
            @pl.when(r < cells)
            def _():
                taps[pl.ds(r * QP * 4 + e, QP, stride=4), :] = rows

            @pl.when(r >= 1)
            def _():
                taps[pl.ds((r - 1) * QP * 4 + 2 + e, QP, stride=4), :] = rows

        return 0

    lax.fori_loop(0, cells + 1, build, 0)
    lane = lax.broadcasted_iota(jnp.int32, (8, 128), 1)
    count = count_ref[0]

    def group(g, _):
        picked = jnp.zeros((8, 128), jnp.float32)
        for n in range(128):
            i = g * 128 + n
            rows = taps[pl.ds(pl.multiple_of(base_ref[i], 4), 8), :]
            picked = jnp.where(lane == n, pltpu.roll(rows, shift_ref[i], 1), picked)
        weights = weight_ref[:, pl.ds(pl.multiple_of(g * 128, 128), 128)]
        value = jnp.sum(picked * weights, axis=0, keepdims=True)
        out_ref[pl.ds(g, 1), :] = jnp.where(lane[0:1, :] + g * 128 < count, value, 0.0)
        return 0

    lax.fori_loop(0, out_ref.shape[0], group, 0)


def shards(
    alm, wig, slot_order, beam, phi_cell, theta_cell, orient_cell_index, tap_weight, sample_count
):
    cube = make_cube(alm, wig, slot_order, beam)
    cells = cube.shape[0] - 1
    samples = phi_cell.shape[0]
    base = (theta_cell * QP + phi_cell) * 4
    shift = (jnp.arange(samples, dtype=jnp.int32) - orient_cell_index) & (PSI - 1)
    smem = pl.BlockSpec(memory_space=pltpu.SMEM)
    vmem = pl.BlockSpec(memory_space=pltpu.VMEM)
    value = pl.pallas_call(
        functools.partial(sample_kernel, cells),
        out_shape=jax.ShapeDtypeStruct((samples // 128, 128), jnp.float32),
        in_specs=[smem, smem, smem, vmem, vmem],
        out_specs=vmem,
        scratch_shapes=[pltpu.VMEM((cells * QP * 4 + 8, 128), jnp.float32)],
        compiler_params=pltpu.CompilerParams(vmem_limit_bytes=24 << 20),
        name="take_samples",
    )(base, shift, sample_count, cube, tap_weight)
    return value.reshape(-1)


def solution(mesh):
    return jax.shard_map(
        shards,
        mesh=mesh,
        in_specs=(
            P(("theta", "phi"), None, None),
            P(("theta", "phi"), None, None),
            P(),
            P(),
            P(("theta", "phi")),
            P(("theta", "phi")),
            P(("theta", "phi")),
            P(None, ("theta", "phi")),
            P(("theta", "phi")),
        ),
        out_specs=P(("theta", "phi")),
        check_vma=False,
    )
```

```python
import functools
import math

import jax
import jax.numpy as jnp
from jax import lax
from jax.experimental import pallas as pl
from jax.experimental.pallas import tpu as pltpu
from jax.sharding import PartitionSpec as P

PSI = 128
PD = 192
RT = 16
QP = 200
CH = 4
PER = RT // CH
MESH = pl.DeviceIdType.MESH
NT = (((1,), (1,)), ((), ()))
TN = (((0,), (0,)), ((), ()))


def slot_m(order, half, m_all):
    stride = max(half // m_all, 1)
    m = lax.shift_right_logical(order * half, m_all.bit_length() - 1)
    if stride > 1:
        m = m + (7 * order) % stride
    return m


def turn_cos(phase, total):
    x = (jnp.abs(phase - total / 2) - total / 4) * (2.0 * math.pi / total)
    x2 = x * x
    p = jnp.float32(-1.0 / math.factorial(11))
    for n in (9, 7, 5, 3, 1):
        p = p * x2 + jnp.float32((-1) ** (n // 2) / math.factorial(n))
    return p * x


def wrap(value, total):
    return value - jnp.floor((value + 0.5) * jnp.float32(1.0 / total)) * total


def psi_rows():
    k_at = lax.broadcasted_iota(jnp.int32, (128, 128), 0)
    p_at = lax.broadcasted_iota(jnp.int32, (128, 128), 1)
    turn = ((k_at * p_at) & (PSI - 1)).astype(jnp.float32)
    scale = 1.0 / math.sqrt(2 * 128)
    psi0 = turn_cos(turn, PSI) * scale
    psi1 = -turn_cos(wrap(turn + 0.75 * PSI, PSI), PSI) * scale
    return psi0.astype(jnp.bfloat16), psi1.astype(jnp.bfloat16), (-psi0).astype(jnp.bfloat16)


def kernel(
    n_theta, n_phi, slots, ldeg, tile, m_all, groups,
    wig_hbm, alm_hbm, beam_hbm, order_hbm, phi_hbm, theta_hbm, orient_hbm, weight_hbm, out_ref,
    wig_v, beam_v, beam_t, alm_v, order_v, cells_v, weight_v, psi_v, sums, x32, x16, landed, grid_v,
    table_v, halo_out, halo_in, taps, index_v, base_s, orient_s,
    wig_sem, in_sem, idx_sem, a_send, a_recv, y_send, y_recv, f_send, f_recv, s_send, s_recv, h_send, h_recv,
):
    me_t = lax.axis_index("theta")
    me_p = lax.axis_index("phi")
    me_y, me_c = me_p // 2, me_p % 2
    n_y = n_phi // 2
    total = PD * n_phi
    rows = PER * 8
    tiles = ldeg // tile
    k_all = n_phi * n_theta * 2 * slots
    per_block = n_theta * 2 * slots

    y_up, y_down, y_far = (me_y + 1) % n_y, (me_y + n_y - 1) % n_y, (me_y + 2) % n_y
    own = me_p
    block = (own, y_down * 2 + me_c, y_up * 2 + me_c, y_far * 2 + me_c)

    def at(t, y, c):
        return (t, y * 2 + c)

    def chunk(n):
        return (3 * n) % CH

    reads = [
        pltpu.make_async_copy(src, dst, in_sem.at[n])
        for n, (src, dst) in enumerate(
            (
                (beam_hbm, beam_v), (alm_hbm, alm_v), (order_hbm, order_v), (phi_hbm, cells_v.at[0]),
                (theta_hbm, cells_v.at[1]), (orient_hbm, cells_v.at[2]), (weight_hbm, weight_v),
            )
        )
    ]

    def wig_copy(n):
        span = pl.ds(pl.multiple_of(n // slots * tile, 128), tile)
        return pltpu.make_async_copy(wig_hbm.at[n % slots, :, span], wig_v.at[n], wig_sem.at[n])

    for r in reads[:3]:
        r.start()

    def wig_start(n, _):
        wig_copy(n).start()
        return 0

    lax.fori_loop(0, slots * tiles, wig_start, 0)
    for r in reads[3:]:
        r.start()

    barrier = pltpu.get_barrier_semaphore()

    def greet(k, _):
        pl.semaphore_signal(
            barrier, inc=1, device_id=at(lax.rem(me_t + k, n_theta), me_y, me_c), device_id_type=MESH
        )
        return 0

    lax.fori_loop(1, n_theta, greet, 0)
    for y, c in ((y_up, me_c), (y_down, me_c), (me_y, 1 - me_c)):
        pl.semaphore_signal(barrier, inc=1, device_id=at(me_t, y, c), device_id_type=MESH)

    psi0, psi1, psi2 = psi_rows()
    psi_v[:128, :128] = psi0
    psi_v[:128, 128:] = psi1
    psi_v[128:, :128] = psi1
    psi_v[128:, 128:] = psi2
    for r in reads[:3]:
        r.wait()

    order_row = order_v[...]
    m_row = slot_m(order_row, total // 2, m_all)
    slot_lane = lax.broadcasted_iota(jnp.int32, (1, m_all), 1)
    eye = (
        lax.broadcasted_iota(jnp.int32, (128, 128), 0) == lax.broadcasted_iota(jnp.int32, (128, 128), 1)
    ).astype(jnp.bfloat16)

    def stage(n, _):
        i, s = n // slots, n % slots

        @pl.when(s == 0)
        def _():
            beam_t[...] = lax.dot_general(
                eye, beam_v[pl.ds(pl.multiple_of(i * tile, 128), tile), :], NT, preferred_element_type=jnp.float32
            ).astype(jnp.bfloat16)

        mine = slot_lane == (me_t * n_phi + me_p) * slots + s
        m_own = jnp.sum(jnp.where(mine, m_row, 0).astype(jnp.float32), axis=1, keepdims=True)
        degree = (lax.broadcasted_iota(jnp.int32, (2, tile), 1) + i * tile).astype(jnp.float32)
        sky = alm_v[s, :, pl.ds(pl.multiple_of(i * tile, 128), tile)].astype(jnp.float32)
        sky = jnp.where(degree >= m_own, sky, 0.0)
        weighted = jnp.concatenate(
            [
                beam_t[...] * jnp.broadcast_to(sky[c:c + 1, :], (128, tile)).astype(jnp.bfloat16)
                for c in range(2)
            ],
            axis=0,
        )
        wig_copy(n).wait()
        term = lax.dot_general(weighted, wig_v[n], NT, preferred_element_type=jnp.float32)

        @pl.when(i == 0)
        def _():
            sums[s] = term

        @pl.when(i > 0)
        def _():
            sums[s] += term

        return 0

    lax.fori_loop(0, slots * tiles, stage, 0)

    def to_psi(s, _):
        x = lax.dot_general(sums[s].astype(jnp.bfloat16), psi_v[...], TN, preferred_element_type=jnp.float32)
        for c in range(2):
            x32[pl.ds(2 * s + c, n_theta * RT, stride=8), :] = x[:, c * 128:(c + 1) * 128]
        return 0

    lax.fori_loop(0, slots, to_psi, 0)

    def narrow(n, _):
        span = pl.ds(pl.multiple_of(n * RT * 8, 16), RT * 8)
        x16[span, :] = x32[span, :].astype(jnp.bfloat16)
        return 0

    lax.fori_loop(0, n_theta, narrow, 0)
    pl.semaphore_wait(barrier, n_theta + 2)

    def x_rows(t, j):
        return pl.ds(pl.multiple_of(t * RT * 8 + j * rows, 16), rows)

    def send(n, _):
        j, k = chunk(n // (n_theta - 1)), n % (n_theta - 1) + 1
        t = lax.rem(me_t + k, n_theta)
        pltpu.make_async_remote_copy(
            src_ref=x16.at[x_rows(t, j), :], dst_ref=landed.at[j, me_t], send_sem=a_send.at[j],
            recv_sem=a_recv.at[j], device_id=at(t, me_y, me_c), device_id_type=MESH,
        ).start()
        return 0

    lax.fori_loop(0, CH * (n_theta - 1), send, 0)

    def landed_all(j):
        others = landed.at[j, pl.ds(0, n_theta - 1)]
        return pltpu.make_async_remote_copy(
            src_ref=others, dst_ref=others, send_sem=a_send.at[j], recv_sem=a_recv.at[j],
            device_id=at(me_t, me_y, 1 - me_c), device_id_type=MESH,
        )

    def share(j, n):
        b = block[n]
        return pltpu.make_async_remote_copy(
            src_ref=grid_v.at[j, b], dst_ref=grid_v.at[j, b], send_sem=s_send.at[j, n], recv_sem=s_recv.at[j, n],
            device_id=at(me_t, me_y, 1 - me_c), device_id_type=MESH,
        )

    def pass_y(j, n):
        return pltpu.make_async_remote_copy(
            src_ref=grid_v.at[j, own], dst_ref=grid_v.at[j, own], send_sem=y_send.at[j, n],
            recv_sem=y_recv.at[j, n], device_id=at(me_t, (y_up, y_down)[n], me_c), device_id_type=MESH,
        )

    def forward(j, n):
        half = pl.ds(n * (PER // 2), PER // 2)
        b = block[1 + n]
        return pltpu.make_async_remote_copy(
            src_ref=grid_v.at[j, b, half], dst_ref=grid_v.at[j, b, half], send_sem=f_send.at[j, n],
            recv_sem=f_recv.at[j, n], device_id=at(me_t, (y_up, y_down)[n], me_c), device_id_type=MESH,
        )

    def gather(n, _):
        j = chunk(n)
        landed[j, me_t] = x16[x_rows(me_t, j), :]
        landed_all(j).wait_recv()
        for pair in range(PER // 2):
            both = landed[j, :, pair * 16:(pair + 1) * 16, :].astype(jnp.float32)
            for h in range(2):
                grid_v[j, own, 2 * pair + h] = (
                    both[:, h * 8:(h + 1) * 8, :].reshape(per_block, 128).astype(jnp.bfloat16)
                )
        pass_y(j, 0).start()
        pass_y(j, 1).start()
        share(j, 0).start()
        return 0

    lax.fori_loop(0, CH, gather, 0)

    m_hi = lax.shift_right_logical(m_row, 4).astype(jnp.float32)
    m_lo = (m_row & 15).astype(jnp.float32)
    split = jnp.concatenate([m_hi, m_lo, jnp.zeros((6, m_all), jnp.float32)], axis=0).astype(jnp.bfloat16)
    col = lax.broadcasted_iota(jnp.int32, (1, per_block), 1)
    slot_col = lax.shift_right_logical(col, 3) * (n_phi * slots) + (lax.shift_right_logical(col, 1) & 3)
    n_at = lax.broadcasted_iota(jnp.int32, (m_all, per_block), 0)
    part_at = (col & 1).astype(jnp.float32)
    q_at = (lax.broadcasted_iota(jnp.int32, (QP, 1), 0) + (me_p * PD - 1 + total)).astype(jnp.float32)

    def table(b, _):
        pick = (n_at == slot_col + b * slots).astype(jnp.bfloat16)
        moved = jnp.dot(split, pick, preferred_element_type=jnp.float32)
        m_col = moved[0:1, :] * 16.0 + moved[1:2, :]
        phase = wrap(m_col * q_at + (1.0 - part_at * 0.25) * total, total)
        table_v[b] = (turn_cos(phase, total) * (1.0 / math.sqrt(m_all))).astype(jnp.bfloat16)
        return 0

    lax.fori_loop(0, n_phi, table, 0)

    for r in reads[3:]:
        r.wait()
    index_v[0] = (cells_v[1] * QP + cells_v[0]) * 4
    index_v[1] = cells_v[2]
    to_smem = [pltpu.make_async_copy(index_v.at[n], dst, idx_sem.at[n]) for n, dst in enumerate((base_s, orient_s))]
    for copy in to_smem:
        copy.start()

    def relay(n, _):
        j = chunk(n)
        for h in range(2):
            pass_y(j, h).wait_recv()
            forward(j, h).start()
            share(j, 1 + h).start()
        return 0

    lax.fori_loop(0, CH, relay, 0)

    def halo(n):
        t = me_t + 1 if n == 0 else me_t + n_theta - 1
        return pltpu.make_async_remote_copy(
            src_ref=halo_out.at[n], dst_ref=halo_in.at[n], send_sem=h_send.at[n], recv_sem=h_recv.at[n],
            device_id=at(lax.rem(t, n_theta), me_y, me_c), device_id_type=MESH,
        )

    def put_taps(cell, b, rows_0, rows_1):
        for e, value in enumerate((rows_0, rows_1)):
            taps[pl.ds(cell * (QP * 4) + 2 * b + e, QP, stride=4), :] = value

    def finish(n):
        j = chunk(n)
        for h in range(4):
            share(j, h).wait_recv()

        def pair_of(pair, _):
            both = None
            for half in range(2):
                picked = [grid_v[j, pl.ds(half * (n_phi // 2), n_phi // 2), 2 * pair + h] for h in range(2)]
                right = jnp.concatenate([p.reshape(k_all // 2, 128) for p in picked], axis=1)
                left = jnp.concatenate([table_v[half * (n_phi // 2) + b] for b in range(n_phi // 2)], axis=1)
                term = jnp.dot(left, right, preferred_element_type=jnp.float32)
                both = term if both is None else both + term
            for h in range(2):
                r = j * PER + 2 * pair + h
                value = both[:, h * 128:(h + 1) * 128]
                turned = pltpu.roll(value, PSI - 1, 1)
                put_taps(r + 1, 0, value, turned)
                put_taps(r, 1, value, turned)

                @pl.when(r == RT - 1)
                def _():
                    halo_out[0] = value

                @pl.when(r == 0)
                def _():
                    halo_out[1] = value

            return 0

        lax.fori_loop(0, PER // 2, pair_of, 0)

        @pl.when(jnp.logical_and(n == 1, me_t < n_theta - 1))
        def _():
            halo(0).start()

        @pl.when(jnp.logical_and(n == 1, me_t > 0))
        def _():
            halo(1).start()

    def far(n, _):
        @pl.when(n < CH)
        def _():
            j = chunk(n)
            forward(j, 0).wait_recv()
            forward(j, 1).wait_recv()
            share(j, 3).start()

        @pl.when(n > 0)
        def _():
            finish(n - 1)

        return 0

    lax.fori_loop(0, CH + 1, far, 0)

    @pl.when(me_t > 0)
    def _():
        halo(0).wait_recv()

    @pl.when(me_t == 0)
    def _():
        halo_in[0] = jnp.zeros((QP, 128), jnp.float32)

    @pl.when(me_t < n_theta - 1)
    def _():
        halo(1).wait_recv()

    @pl.when(me_t == n_theta - 1)
    def _():
        halo_in[1] = jnp.zeros((QP, 128), jnp.float32)

    for n in range(2):
        value = halo_in[n]
        put_taps(n * RT, n, value, pltpu.roll(value, PSI - 1, 1))

    for copy in to_smem:
        copy.wait()
    lane = lax.broadcasted_iota(jnp.int32, (8, 128), 1)

    def group(g, _):
        picked = jnp.zeros((8, 128), jnp.float32)
        for n in range(128):
            eight = taps[pl.ds(base_s[g, n], 8), :]
            tap = jnp.sum(jnp.where(lane == orient_s[g, n], eight, 0.0), axis=1, keepdims=True)
            picked = jnp.where(lane == n, tap, picked)
        weights = weight_v[:, pl.ds(pl.multiple_of(g * 128, 128), 128)]
        out_ref[pl.ds(g, 1), :] = jnp.sum(picked * weights, axis=0, keepdims=True)
        return 0

    lax.fori_loop(0, groups, group, 0)

    @pl.when(me_t < n_theta - 1)
    def _():
        halo(0).wait_send()

    @pl.when(me_t > 0)
    def _():
        halo(1).wait_send()

    def drain(j, _):
        landed_all(j).wait_send()
        for h in range(2):
            pass_y(j, h).wait_send()
            forward(j, h).wait_send()
        for h in range(4):
            share(j, h).wait_send()
        return 0

    lax.fori_loop(0, CH, drain, 0)


def shards(
    alm, wig, slot_order, beam, phi_cell, theta_cell, orient_cell_index, tap_weight, sample_count
):
    n_theta, n_phi = lax.axis_size("theta"), lax.axis_size("phi")
    slots, _, ldeg = alm.shape
    m_all = slot_order.shape[0]
    tile = min(ldeg // 2, 4096)
    tiles = ldeg // tile
    k_block = n_theta * 2 * slots
    groups = phi_cell.shape[0] // 128
    cells = [c.reshape(groups, 128) for c in (phi_cell, theta_cell, orient_cell_index)]
    anywhere = pl.BlockSpec(memory_space=pl.ANY)
    dma = pltpu.SemaphoreType.DMA
    f32, bf16, i32 = jnp.float32, jnp.bfloat16, jnp.int32
    value = pl.pallas_call(
        functools.partial(kernel, n_theta, n_phi, slots, ldeg, tile, m_all, groups),
        out_shape=jax.ShapeDtypeStruct((groups, 128), f32),
        in_specs=[anywhere] * 8,
        out_specs=pl.BlockSpec(memory_space=pltpu.VMEM),
        scratch_shapes=[
            pltpu.VMEM((slots * tiles, wig.shape[1], tile), bf16),
            pltpu.VMEM(beam.shape, bf16),
            pltpu.VMEM((128, tile), bf16),
            pltpu.VMEM(alm.shape, bf16),
            pltpu.VMEM((1, m_all), i32),
            pltpu.VMEM((3, groups, 128), i32),
            pltpu.VMEM(tap_weight.shape, f32),
            pltpu.VMEM((256, 256), bf16),
            pltpu.VMEM((slots, 256, n_theta * RT), f32),
            pltpu.VMEM((n_theta * RT * 8, 128), f32),
            pltpu.VMEM((n_theta * RT * 8, 128), bf16),
            pltpu.VMEM((CH, n_theta, PER * 8, 128), bf16),
            pltpu.VMEM((CH, n_phi, PER, k_block, 128), bf16),
            pltpu.VMEM((n_phi, QP, k_block), bf16),
            pltpu.VMEM((2, QP, 128), f32),
            pltpu.VMEM((2, QP, 128), f32),
            pltpu.VMEM(((RT + 1) * QP * 4 + 8, 128), f32),
            pltpu.VMEM((2, groups, 128), i32),
            pltpu.SMEM((groups, 128), i32),
            pltpu.SMEM((groups, 128), i32),
            dma((slots * tiles,)), dma((7,)), dma((2,)),
            dma((CH,)), dma((CH,)),
            dma((CH, 2)), dma((CH, 2)),
            dma((CH, 2)), dma((CH, 2)),
            dma((CH, 4)), dma((CH, 4)),
            dma((2,)), dma((2,)),
        ],
        compiler_params=pltpu.CompilerParams(
            collective_id=0, has_side_effects=True, vmem_limit_bytes=58 << 20
        ),
        name="convolve",
    )(wig, alm, beam, slot_order.reshape(1, -1), *cells, tap_weight)
    live = jnp.arange(phi_cell.shape[0], dtype=jnp.int32) < sample_count[0]
    return jnp.where(live, value.reshape(-1), jnp.float32(0.0))


def solution(mesh):
    return jax.shard_map(
        shards,
        mesh=mesh,
        in_specs=(
            P(("theta", "phi"), None, None),
            P(("theta", "phi"), None, None),
            P(),
            P(),
            P(("theta", "phi")),
            P(("theta", "phi")),
            P(("theta", "phi")),
            P(None, ("theta", "phi")),
            P(("theta", "phi")),
        ),
        out_specs=P(("theta", "phi")),
        check_vma=False,
    )
```

```python
import functools
import math

import jax
import jax.numpy as jnp
from jax import lax
from jax.experimental import pallas as pl
from jax.experimental.pallas import tpu as pltpu
from jax.sharding import PartitionSpec as P

PSI = 128
PD = 192
RT = 16
QP = 208
HALF = RT // 2
MESH = pl.DeviceIdType.MESH
NT = (((1,), (1,)), ((), ()))
TN = (((0,), (0,)), ((), ()))


def slot_m(order, half, m_all):
    stride = max(half // m_all, 1)
    m = lax.shift_right_logical(order * half, m_all.bit_length() - 1)
    if stride > 1:
        m = m + (7 * order) % stride
    return m


def turn_cos(phase, total):
    x = (jnp.abs(phase - total / 2) - total / 4) * (2.0 * math.pi / total)
    x2 = x * x
    p = jnp.float32(-1.0 / math.factorial(11))
    for n in (9, 7, 5, 3, 1):
        p = p * x2 + jnp.float32((-1) ** (n // 2) / math.factorial(n))
    return p * x


def wrap(value, total):
    return value - jnp.floor((value + 0.5) * jnp.float32(1.0 / total)) * total


def psi_rows():
    k_at = lax.broadcasted_iota(jnp.int32, (128, 128), 0)
    p_at = lax.broadcasted_iota(jnp.int32, (128, 128), 1)
    turn = ((k_at * p_at) & (PSI - 1)).astype(jnp.float32)
    scale = 1.0 / math.sqrt(2 * 128)
    psi0 = turn_cos(turn, PSI) * scale
    psi1 = -turn_cos(wrap(turn + 0.75 * PSI, PSI), PSI) * scale
    return psi0.astype(jnp.bfloat16), psi1.astype(jnp.bfloat16), (-psi0).astype(jnp.bfloat16)


def kernel(
    n_theta, n_phi, slots, ldeg, tile, m_all, groups,
    wig_hbm, alm_hbm, beam_hbm, order_hbm, phi_hbm, theta_hbm, orient_hbm, weight_hbm, out_ref,
    wig_v, beam_v, beam_t, alm_v, order_v, cells_v, weight_v, psi_v, sums, x32, x16, landed, spread, grid_v,
    table_v, part_v, share_out, share_in, halo_out, halo_in, taps, index_v,
    base_s, orient_s, wig_sem, in_sem, idx_sem, a_send, a_recv, y_send, y_recv, f_send, f_recv, s_send, s_recv, h_send, h_recv,
):
    me_t = lax.axis_index("theta")
    me_p = lax.axis_index("phi")
    me_y, me_c = me_p // 2, me_p % 2
    n_y = n_phi // 2
    total = PD * n_phi
    tiles = ldeg // tile
    sources = 2 * n_theta
    span = HALF * 4
    per_block = 4 * sources
    pairs = HALF // 2
    y_up, y_down, y_far = (me_y + 1) % n_y, (me_y + n_y - 1) % n_y, (me_y + 2) % n_y

    def at(t, y, c):
        return (t, y * 2 + c)

    reads = [
        pltpu.make_async_copy(src, dst, in_sem.at[n])
        for n, (src, dst) in enumerate(
            (
                (beam_hbm, beam_v), (alm_hbm, alm_v), (order_hbm, order_v), (phi_hbm, cells_v.at[0]),
                (theta_hbm, cells_v.at[1]), (orient_hbm, cells_v.at[2]), (weight_hbm, weight_v),
            )
        )
    ]

    def place(n):
        sh, i, s2 = n // (2 * tiles), n // 2 % tiles, n % 2
        return sh * 2 + s2, i

    def wig_copy(n):
        s, i = place(n)
        return pltpu.make_async_copy(
            wig_hbm.at[s, :, pl.ds(pl.multiple_of(i * tile, 128), tile)], wig_v.at[n], wig_sem.at[n]
        )

    for r in reads[:3]:
        r.start()

    def wig_start(n, _):
        wig_copy(n).start()
        return 0

    lax.fori_loop(0, slots * tiles, wig_start, 0)
    for r in reads[3:]:
        r.start()

    def target(n):
        return (me_t + (n + 1) // 2) % n_theta, (me_c + n + 1) % 2

    barrier = pltpu.get_barrier_semaphore()

    def greet(n, _):
        t, c = target(n)
        pl.semaphore_signal(barrier, inc=1, device_id=at(t, me_y, c), device_id_type=MESH)
        return 0

    others = sources - 1
    lax.fori_loop(0, others, greet, 0)
    for y in (y_up, y_down):
        pl.semaphore_signal(barrier, inc=1, device_id=at(me_t, y, me_c), device_id_type=MESH)

    psi0, psi1, psi2 = psi_rows()
    psi_v[:128, :128] = psi0
    psi_v[:128, 128:] = psi1
    psi_v[128:, :128] = psi1
    psi_v[128:, 128:] = psi2
    for r in reads[:3]:
        r.wait()

    m_row = slot_m(order_v[...], total // 2, m_all)
    slot_lane = lax.broadcasted_iota(jnp.int32, (1, m_all), 1)
    eye = (
        lax.broadcasted_iota(jnp.int32, (128, 128), 0) == lax.broadcasted_iota(jnp.int32, (128, 128), 1)
    ).astype(jnp.bfloat16)

    def stage(n, _):
        s, i = place(n)

        @pl.when(jnp.logical_and(n < 2 * tiles, n % 2 == 0))
        def _():
            beam_t[i] = lax.dot_general(
                eye, beam_v[pl.ds(pl.multiple_of(i * tile, 128), tile), :], NT, preferred_element_type=jnp.float32
            ).astype(jnp.bfloat16)

        mine = slot_lane == (me_t * n_phi + me_p) * slots + s
        m_own = jnp.sum(jnp.where(mine, m_row, 0).astype(jnp.float32), axis=1, keepdims=True)
        degree = (lax.broadcasted_iota(jnp.int32, (2, tile), 1) + i * tile).astype(jnp.float32)
        sky = alm_v[s, :, pl.ds(pl.multiple_of(i * tile, 128), tile)].astype(jnp.float32)
        sky = jnp.where(degree >= m_own, sky, 0.0)
        weighted = jnp.concatenate(
            [
                beam_t[i] * jnp.broadcast_to(sky[c:c + 1, :], (128, tile)).astype(jnp.bfloat16)
                for c in range(2)
            ],
            axis=0,
        )
        wig_copy(n).wait()
        term = lax.dot_general(weighted, wig_v[n], NT, preferred_element_type=jnp.float32)

        @pl.when(i == 0)
        def _():
            sums[n % 2] = term

        @pl.when(i > 0)
        def _():
            sums[n % 2] += term

        return 0

    def quad_at(q, c):
        return q + c * (1 - 2 * q)

    def quad_rows(t, c, q):
        return pl.ds(pl.multiple_of((t * 2 + c) * span + quad_at(q, c) * 16, 16), 16)

    def send_half(sh, _):
        lax.fori_loop(sh * 2 * tiles, (sh + 1) * 2 * tiles, stage, 0)

        def to_psi(s2, _):
            x = lax.dot_general(sums[s2].astype(jnp.bfloat16), psi_v[...], TN, preferred_element_type=jnp.float32)
            for c in range(2):
                x32[pl.ds(2 * s2 + c, n_theta * RT, stride=4), :] = x[:, c * 128:(c + 1) * 128]
            return 0

        lax.fori_loop(0, 2, to_psi, 0)

        def narrow(n, _):
            rows = pl.ds(pl.multiple_of(n * RT * 4, 16), RT * 4)
            x16[sh, rows, :] = x32[rows, :].astype(jnp.bfloat16)
            return 0

        lax.fori_loop(0, n_theta, narrow, 0)

        @pl.when(sh == 0)
        def _():
            pl.semaphore_wait(barrier, others + 2)

        def send(n, _):
            q = n // others
            t, c = target(n % others)
            pltpu.make_async_remote_copy(
                src_ref=x16.at[sh, quad_rows(t, c, q), :], dst_ref=landed.at[sh, q, me_t * 2 + me_c],
                send_sem=a_send.at[sh, q], recv_sem=a_recv.at[sh, q],
                device_id=at(t, me_y, c), device_id_type=MESH,
            ).start()
            return 0

        lax.fori_loop(0, 2 * others, send, 0)
        for q in range(2):
            landed[sh, q, me_t * 2 + me_c] = x16[sh, quad_rows(me_t, me_c, q), :]
        return 0

    lax.fori_loop(0, 2, send_half, 0)

    def arrived(sh, q):
        block = landed.at[sh, q, pl.ds(0, others)]
        return pltpu.make_async_remote_copy(
            src_ref=block, dst_ref=block, send_sem=a_send.at[sh, q], recv_sem=a_recv.at[sh, q],
            device_id=at(me_t, me_y, 1 - me_c), device_id_type=MESH,
        )

    def pass_y(sh, q, h):
        block = grid_v.at[sh, me_y, pl.ds(quad_at(q, me_c) * 4, 4)]
        return pltpu.make_async_remote_copy(
            src_ref=block, dst_ref=block, send_sem=y_send.at[sh, q, h], recv_sem=y_recv.at[sh, q, h],
            device_id=at(me_t, (y_up, y_down)[h], me_c), device_id_type=MESH,
        )

    def forward(sh, q, h):
        block = grid_v.at[sh, (y_down, y_up)[h], pl.ds(quad_at(q, me_c) * 4 + 2 * h, 2)]
        return pltpu.make_async_remote_copy(
            src_ref=block, dst_ref=block, send_sem=f_send.at[sh, q, h], recv_sem=f_recv.at[sh, q, h],
            device_id=at(me_t, (y_up, y_down)[h], me_c), device_id_type=MESH,
        )

    def gather(sh, q):
        arrived(sh, q).wait_recv()
        spread[...] = landed[sh, q].astype(jnp.float32).reshape(sources * 16, 128)
        first = quad_at(q, me_c) * 4

        def cycle(r, _):
            for p in range(4):
                grid_v[sh, me_y, first + r, p * sources:(p + 1) * sources, :] = spread[
                    pl.ds(r * 4 + p, sources, stride=16), :
                ].astype(jnp.bfloat16)
            return 0

        lax.fori_loop(0, 4, cycle, 0)
        pass_y(sh, q, 0).start()
        pass_y(sh, q, 1).start()

    def relay(sh, q):
        for h in range(2):
            pass_y(sh, q, h).wait_recv()
            forward(sh, q, h).start()

    def far(sh, q):
        for h in range(2):
            forward(sh, q, h).wait_recv()

    gather(0, 0)
    gather(0, 1)

    m_hi = lax.shift_right_logical(m_row, 4).astype(jnp.float32)
    m_lo = (m_row & 15).astype(jnp.float32)
    split = jnp.concatenate([m_hi, m_lo, jnp.zeros((6, m_all), jnp.float32)], axis=0).astype(jnp.bfloat16)
    col = lax.broadcasted_iota(jnp.int32, (1, per_block), 1)
    part = col // sources
    source = col % sources
    slot_col = (source // 2 * n_phi + source % 2) * slots + part // 2
    n_at = lax.broadcasted_iota(jnp.int32, (m_all, per_block), 0)
    part_at = (part % 2).astype(jnp.float32)
    row = lax.broadcasted_iota(jnp.int32, (2 * QP, 1), 0)
    sibling = me_y * 2 + 1 - me_c
    q_at = jnp.where(row < QP, row + me_p * PD, row - QP + sibling * PD) - 1 + total
    q_at = q_at.astype(jnp.float32)

    def table(n, _):
        sh, b = n // n_y, n % n_y
        pick = (n_at == slot_col + (b * 2 * slots + sh * 2)).astype(jnp.bfloat16)
        moved = jnp.dot(split, pick, preferred_element_type=jnp.float32)
        m_col = moved[0:1, :] * 16.0 + moved[1:2, :]
        phase = wrap(m_col * q_at + (1.0 - part_at * 0.25) * total, total)
        table_v[sh, :, pl.ds(pl.multiple_of(b * per_block, per_block), per_block)] = (
            turn_cos(phase, total) * (1.0 / math.sqrt(m_all))
        ).astype(jnp.bfloat16)
        return 0

    lax.fori_loop(0, 2 * n_y, table, 0)

    for r in reads[3:]:
        r.wait()
    index_v[0] = (cells_v[1] * QP + cells_v[0]) * 4
    index_v[1] = cells_v[2]
    to_smem = [pltpu.make_async_copy(index_v.at[n], dst, idx_sem.at[n]) for n, dst in enumerate((base_s, orient_s))]
    for copy in to_smem:
        copy.start()

    def product(sh, pair):
        right = jnp.concatenate(
            [grid_v[sh, :, 2 * pair + h].reshape(n_y * per_block, 128) for h in range(2)], axis=1
        )
        return jnp.dot(table_v[sh], right, preferred_element_type=jnp.float32)

    relay(0, 0)
    gather(1, 0)
    relay(0, 1)
    gather(1, 1)

    def first_part(pair, _):
        part_v[pair] = product(0, pair)
        return 0

    far(0, 0)
    far(0, 1)
    relay(1, 0)
    lax.fori_loop(0, pairs // 2, first_part, 0)
    relay(1, 1)
    lax.fori_loop(pairs // 2, pairs, first_part, 0)

    def share(n):
        return pltpu.make_async_remote_copy(
            src_ref=share_out.at[n], dst_ref=share_in.at[n], send_sem=s_send.at[n], recv_sem=s_recv.at[n],
            device_id=at(me_t, me_y, 1 - me_c), device_id_type=MESH,
        )

    def halo(n):
        t = (me_t + n_theta - 1 + 2 * me_c) % n_theta
        return pltpu.make_async_remote_copy(
            src_ref=halo_out.at[n], dst_ref=halo_in.at[1 - me_c], send_sem=h_send.at[n], recv_sem=h_recv.at[1 - me_c],
            device_id=at(t, me_y, (me_c + n) % 2), device_id_type=MESH,
        )

    edge_goes = jnp.logical_or(
        jnp.logical_and(me_c == 0, me_t > 0), jnp.logical_and(me_c == 1, me_t < n_theta - 1)
    )

    def put_taps(cell, b, value):
        for e, rows in enumerate((value, pltpu.roll(value, PSI - 1, 1))):
            taps[pl.ds(cell * (QP * 4) + 2 * b + e, QP, stride=4), :] = rows

    def put_cycle(r, value):
        turned = pltpu.roll(value, PSI - 1, 1)
        for cell, b in ((r + 1, 0), (r, 1)):
            for e, rows in enumerate((value, turned)):
                taps[pl.ds(cell * (QP * 4) + 2 * b + e, QP, stride=4), :] = rows

    def pair_at(n, c):
        return n + c * (pairs - 1 - 2 * n)

    def finish(n, _):
        pair = pair_at(n, me_c)

        @pl.when(n % 2 == 0)
        def _():
            far(1, n // 2)

        both = product(1, pair) + part_v[pair]
        for h in range(2):
            share_out[n, h] = both[QP:, h * 128:(h + 1) * 128].astype(jnp.bfloat16)
        share(n).start()

        @pl.when(n == 0)
        def _():
            for i in range(2):
                rows = both[i * QP:(i + 1) * QP]
                halo_out[i] = jnp.where(me_c == 0, rows[:, :128], rows[:, 128:]).astype(jnp.bfloat16)

        @pl.when(jnp.logical_and(n == 0, edge_goes))
        def _():
            halo(0).start()
            halo(1).start()

        for h in range(2):
            put_cycle(me_c * HALF + 2 * pair + h, both[:QP, h * 128:(h + 1) * 128])
        return 0

    lax.fori_loop(0, pairs, finish, 0)

    def take_share(n, _):
        share(n).wait_recv()
        for h in range(2):
            put_cycle((1 - me_c) * HALF + 2 * pair_at(n, 1 - me_c) + h, share_in[n, h].astype(jnp.float32))
        return 0

    lax.fori_loop(0, pairs, take_share, 0)

    def edge_in(slot):
        return pltpu.make_async_remote_copy(
            src_ref=halo_out.at[0], dst_ref=halo_in.at[slot], send_sem=h_send.at[0], recv_sem=h_recv.at[slot],
            device_id=at(me_t, me_y, 1 - me_c), device_id_type=MESH,
        )

    for slot, at_end in ((0, me_t == 0), (1, me_t == n_theta - 1)):
        @pl.when(jnp.logical_not(at_end))
        def _():
            edge_in(slot).wait_recv()

        @pl.when(at_end)
        def _():
            halo_in[slot] = jnp.zeros((QP, 128), jnp.bfloat16)

        put_taps(slot * RT, slot, halo_in[slot].astype(jnp.float32))

    for copy in to_smem:
        copy.wait()
    lane = lax.broadcasted_iota(jnp.int32, (8, 128), 1)

    def group(g, _):
        picked = jnp.zeros((8, 128), jnp.float32)
        for n in range(128):
            eight = taps[pl.ds(base_s[g, n], 8), :]
            tap = jnp.sum(jnp.where(lane == orient_s[g, n], eight, 0.0), axis=1, keepdims=True)
            picked = jnp.where(lane == n, tap, picked)
        weights = weight_v[:, pl.ds(pl.multiple_of(g * 128, 128), 128)]
        out_ref[pl.ds(g, 1), :] = jnp.sum(picked * weights, axis=0, keepdims=True)
        return 0

    lax.fori_loop(0, groups, group, 0)

    @pl.when(edge_goes)
    def _():
        halo(0).wait_send()
        halo(1).wait_send()

    def drain(sh, _):
        for q in range(2):
            arrived(sh, q).wait_send()
            for h in range(2):
                pass_y(sh, q, h).wait_send()
                forward(sh, q, h).wait_send()
        return 0

    lax.fori_loop(0, 2, drain, 0)

    def drain_share(n, _):
        share(n).wait_send()
        return 0

    lax.fori_loop(0, pairs, drain_share, 0)


def shards(
    alm, wig, slot_order, beam, phi_cell, theta_cell, orient_cell_index, tap_weight, sample_count
):
    n_theta, n_phi = lax.axis_size("theta"), lax.axis_size("phi")
    slots, _, ldeg = alm.shape
    m_all = slot_order.shape[0]
    tile = min(ldeg // 2, 4096)
    tiles = ldeg // tile
    n_y = n_phi // 2
    sources = 2 * n_theta
    block = 4 * sources
    pairs = HALF // 2
    groups = phi_cell.shape[0] // 128
    cells = [c.reshape(groups, 128) for c in (phi_cell, theta_cell, orient_cell_index)]
    anywhere = pl.BlockSpec(memory_space=pl.ANY)
    dma = pltpu.SemaphoreType.DMA
    f32, bf16, i32 = jnp.float32, jnp.bfloat16, jnp.int32
    value = pl.pallas_call(
        functools.partial(kernel, n_theta, n_phi, slots, ldeg, tile, m_all, groups),
        out_shape=jax.ShapeDtypeStruct((groups, 128), f32),
        in_specs=[anywhere] * 8,
        out_specs=pl.BlockSpec(memory_space=pltpu.VMEM),
        scratch_shapes=[
            pltpu.VMEM((slots * tiles, wig.shape[1], tile), bf16),
            pltpu.VMEM(beam.shape, bf16),
            pltpu.VMEM((tiles, 128, tile), bf16),
            pltpu.VMEM(alm.shape, bf16),
            pltpu.VMEM((1, m_all), i32),
            pltpu.VMEM((3, groups, 128), i32),
            pltpu.VMEM(tap_weight.shape, f32),
            pltpu.VMEM((256, 256), bf16),
            pltpu.VMEM((2, 256, n_theta * RT), f32),
            pltpu.VMEM((n_theta * RT * 4, 128), f32),
            pltpu.VMEM((2, n_theta * RT * 4, 128), bf16),
            pltpu.VMEM((2, 2, sources, 16, 128), bf16),
            pltpu.VMEM((sources * 16, 128), f32),
            pltpu.VMEM((2, n_y, HALF, block, 128), bf16),
            pltpu.VMEM((2, 2 * QP, n_y * block), bf16),
            pltpu.VMEM((pairs, 2 * QP, 256), f32),
            pltpu.VMEM((pairs, 2, QP, 128), bf16),
            pltpu.VMEM((pairs, 2, QP, 128), bf16),
            pltpu.VMEM((2, QP, 128), bf16),
            pltpu.VMEM((2, QP, 128), bf16),
            pltpu.VMEM(((RT + 1) * QP * 4 + 8, 128), f32),
            pltpu.VMEM((2, groups, 128), i32),
            pltpu.SMEM((groups, 128), i32),
            pltpu.SMEM((groups, 128), i32),
            dma((slots * tiles,)), dma((7,)), dma((2,)),
            dma((2, 2)), dma((2, 2)),
            dma((2, 2, 2)), dma((2, 2, 2)),
            dma((2, 2, 2)), dma((2, 2, 2)),
            dma((pairs,)), dma((pairs,)),
            dma((2,)), dma((2,)),
        ],
        compiler_params=pltpu.CompilerParams(
            collective_id=0, has_side_effects=True, vmem_limit_bytes=58 << 20
        ),
        name="convolve",
    )(wig, alm, beam, slot_order.reshape(1, -1), *cells, tap_weight)
    live = jnp.arange(phi_cell.shape[0], dtype=jnp.int32) < sample_count[0]
    return jnp.where(live, value.reshape(-1), jnp.float32(0.0))


def solution(mesh):
    return jax.shard_map(
        shards,
        mesh=mesh,
        in_specs=(
            P(("theta", "phi"), None, None),
            P(("theta", "phi"), None, None),
            P(),
            P(),
            P(("theta", "phi")),
            P(("theta", "phi")),
            P(("theta", "phi")),
            P(None, ("theta", "phi")),
            P(("theta", "phi")),
        ),
        out_specs=P(("theta", "phi")),
        check_vma=False,
    )
```

```python
import functools
import math

import jax
import jax.numpy as jnp
from jax import lax
from jax.experimental import pallas as pl
from jax.experimental.pallas import tpu as pltpu
from jax.sharding import PartitionSpec as P

PSI = 128
PD = 192
RT = 16
QP = 208
HALF = RT // 2
MESH = pl.DeviceIdType.MESH
NT = (((1,), (1,)), ((), ()))


def slot_m(order, half, m_all):
    stride = max(half // m_all, 1)
    m = lax.shift_right_logical(order * half, m_all.bit_length() - 1)
    if stride > 1:
        m = m + (7 * order) % stride
    return m


def turn_cos(phase, total):
    x = (jnp.abs(phase - total / 2) - total / 4) * (2.0 * math.pi / total)
    x2 = x * x
    p = jnp.float32(-1.0 / math.factorial(11))
    for n in (9, 7, 5, 3, 1):
        p = p * x2 + jnp.float32((-1) ** (n // 2) / math.factorial(n))
    return p * x


def wrap(value, total):
    return value - jnp.floor((value + 0.5) * jnp.float32(1.0 / total)) * total


def psi_rows():
    k_at = lax.broadcasted_iota(jnp.int32, (128, 128), 0)
    p_at = lax.broadcasted_iota(jnp.int32, (128, 128), 1)
    turn = ((k_at * p_at) & (PSI - 1)).astype(jnp.float32)
    scale = 1.0 / math.sqrt(2 * 128)
    psi0 = turn_cos(turn, PSI) * scale
    psi1 = -turn_cos(wrap(turn + 0.75 * PSI, PSI), PSI) * scale
    return psi0.astype(jnp.bfloat16), psi1.astype(jnp.bfloat16), (-psi0).astype(jnp.bfloat16)


def kernel(
    n_theta, n_phi, slots, ldeg, tile, m_all, groups,
    wig_hbm, alm_hbm, beam_hbm, order_hbm, phi_hbm, theta_hbm, orient_hbm, weight_hbm, count_hbm, out_ref,
    wig_v, beam_v, beam_t, alm_v, sky_v, order_v, cells_v, weight_v, psi_v, sums, x32, x16, landed, spread, grid_v,
    table_v, part_v, share_out, share_in, halo_out, halo_in, taps, index_v,
    base_s, orient_s, count_s, wig_sem, beam_sem, in_sem, idx_sem, a_send, a_recv, y_send, y_recv, f_send, f_recv, s_send, s_recv, h_send, h_recv,
):
    me_t = lax.axis_index("theta")
    me_p = lax.axis_index("phi")
    me_y, me_c = me_p // 2, me_p % 2
    n_y = n_phi // 2
    total = PD * n_phi
    tiles = ldeg // tile
    sources = 2 * n_theta
    bunch = sources // 4
    span = HALF * 4
    per_block = 4 * bunch
    wide = n_y * per_block
    pairs = HALF // 2
    y_up, y_down, y_far = (me_y + 1) % n_y, (me_y + n_y - 1) % n_y, (me_y + 2) % n_y

    def at(t, y, c):
        return (t, y * 2 + c)

    reads = [
        pltpu.make_async_copy(src, dst, in_sem.at[n])
        for n, (src, dst) in enumerate(
            (
                (alm_hbm, alm_v), (order_hbm, order_v), (count_hbm, count_s), (phi_hbm, cells_v.at[0]),
                (theta_hbm, cells_v.at[1]), (orient_hbm, cells_v.at[2]), (weight_hbm, weight_v),
            )
        )
    ]

    def place(n):
        sh, i, s2 = n // (2 * tiles), n // 2 % tiles, n % 2
        return sh * 2 + s2, i

    def wig_copy(n):
        s, i = place(n)
        return pltpu.make_async_copy(
            wig_hbm.at[s, :, pl.ds(pl.multiple_of(i * tile, 128), tile)], wig_v.at[n], wig_sem.at[n]
        )

    def beam_copy(i):
        part = pl.ds(pl.multiple_of(i * tile, 128), tile)
        return pltpu.make_async_copy(beam_hbm.at[part, :], beam_v.at[part, :], beam_sem.at[i])

    for r in reads[:2]:
        r.start()
    for i in range(tiles):
        beam_copy(i).start()

    def wig_start(n, _):
        wig_copy(n).start()
        return 0

    lax.fori_loop(0, 2 * tiles, wig_start, 0)
    for r in reads[2:]:
        r.start()

    def target(n):
        m = n + 5 * sources // 8
        return (me_t + m // 2) & (n_theta - 1), (me_c + m) & 1

    barrier = pltpu.get_barrier_semaphore()

    def greet(n, _):
        t, c = target(n)

        @pl.when(n != alone)
        def _():
            pl.semaphore_signal(barrier, inc=1, device_id=at(t, me_y, c), device_id_type=MESH)

        return 0

    others = sources - 1
    alone = sources - 5 * sources // 8
    lax.fori_loop(0, sources, greet, 0)
    for y in (y_up, y_down):
        pl.semaphore_signal(barrier, inc=1, device_id=at(me_t, y, me_c), device_id_type=MESH)

    psi0, psi1, psi2 = psi_rows()
    psi_v[:128, :128] = psi0
    psi_v[:128, 128:] = psi1
    psi_v[128:, :128] = psi1
    psi_v[128:, 128:] = psi2
    for r in reads[:2]:
        r.wait()

    m_row = slot_m(order_v[...], total // 2, m_all)
    slot_lane = lax.broadcasted_iota(jnp.int32, (1, m_all), 1)
    eye = (
        lax.broadcasted_iota(jnp.int32, (128, 128), 0) == lax.broadcasted_iota(jnp.int32, (128, 128), 1)
    ).astype(jnp.bfloat16)

    m_hi = lax.shift_right_logical(m_row, 4).astype(jnp.float32)
    m_lo = (m_row & 15).astype(jnp.float32)
    split = jnp.concatenate([m_hi, m_lo, jnp.zeros((6, m_all), jnp.float32)], axis=0).astype(jnp.bfloat16)
    col = lax.broadcasted_iota(jnp.int32, (1, wide), 1)
    part = col % per_block // bunch
    source = col % bunch
    slot_col = (source // 2 * n_phi + col // per_block * 2 + source % 2) * slots + part // 2
    n_at = lax.broadcasted_iota(jnp.int32, (m_all, wide), 0)
    part_at = (part % 2).astype(jnp.float32)
    row = lax.broadcasted_iota(jnp.int32, (2 * QP, 1), 0)
    sibling = me_y * 2 + 1 - me_c
    q_at = jnp.where(row < QP, row + me_p * PD, row - QP + sibling * PD) - 1 + total
    q_at = q_at.astype(jnp.float32)

    def table(n, _):
        sh, g = n // 4, n % 4
        first = g * (n_theta // 4) * n_phi * slots + sh * 2
        pick = (n_at == slot_col + first).astype(jnp.bfloat16)
        moved = jnp.dot(split, pick, preferred_element_type=jnp.float32)
        m_col = moved[0:1, :] * 16.0 + moved[1:2, :]
        phase = wrap(m_col * q_at + (1.0 - part_at * 0.25) * total, total)
        table_v[sh, :, pl.ds(pl.multiple_of(g * wide, wide), wide)] = (
            turn_cos(phase, total) * (1.0 / math.sqrt(m_all))
        ).astype(jnp.bfloat16)
        return 0

    def turn_beam(i, _):
        beam_copy(i).wait()
        beam_t[i] = lax.dot_general(
            eye, beam_v[pl.ds(pl.multiple_of(i * tile, 128), tile), :], NT, preferred_element_type=jnp.float32
        ).astype(jnp.bfloat16)
        return 0

    def mask_sky(s, _):
        mine = slot_lane == (me_t * n_phi + me_p) * slots + s
        m_own = jnp.sum(jnp.where(mine, m_row, 0).astype(jnp.float32), axis=1, keepdims=True)
        degree = lax.broadcasted_iota(jnp.int32, (2, ldeg), 1).astype(jnp.float32)
        sky = jnp.where(degree >= m_own, alm_v[s].astype(jnp.float32), 0.0)
        for c in range(2):
            sky_v[s, c] = jnp.broadcast_to(sky[c:c + 1, :], (16, ldeg)).astype(jnp.bfloat16)
        return 0

    lax.fori_loop(0, slots, mask_sky, 0)
    lax.fori_loop(0, tiles, turn_beam, 0)

    def stage(n, _):
        s, i = place(n)
        part = beam_t[i].reshape(8, 16, tile)
        span_i = pl.ds(pl.multiple_of(i * tile, 128), tile)
        weighted = jnp.concatenate(
            [(part * sky_v[s, c, :, span_i][None]).reshape(128, tile) for c in range(2)], axis=0
        )
        wig_copy(n).wait()

        @pl.when(n < (slots - 2) * tiles)
        def _():
            wig_copy(n + 2 * tiles).start()

        term = lax.dot_general(wig_v[n], weighted, NT, preferred_element_type=jnp.float32)

        @pl.when(i == 0)
        def _():
            sums[n % 2] = term

        @pl.when(i > 0)
        def _():
            sums[n % 2] += term

        return 0

    def rows_of(t, c):
        return pl.ds(pl.multiple_of((t * 2 + c) * span, 16), span)

    def send_half(sh):
        def to_psi(s2, _):
            x = jnp.dot(sums[s2].astype(jnp.bfloat16), psi_v[...], preferred_element_type=jnp.float32)
            for c in range(2):
                x32[pl.ds(2 * s2 + c, n_theta * RT, stride=4), :] = x[:, c * 128:(c + 1) * 128]
            return 0

        lax.fori_loop(0, 2, to_psi, 0)

        x16[sh] = x32[...].astype(jnp.bfloat16)

        if sh == 0:
            pl.semaphore_wait(barrier, others + 2)

        def send(n, _):
            t, c = target(n)

            @pl.when(n != alone)
            def _():
                pltpu.make_async_remote_copy(
                    src_ref=x16.at[sh, rows_of(t, c), :], dst_ref=landed.at[sh, me_t * 2 + me_c],
                    send_sem=a_send.at[sh], recv_sem=a_recv.at[sh, me_t // (n_theta // 4)],
                    device_id=at(t, me_y, c), device_id_type=MESH,
                ).start()

            return 0

        lax.fori_loop(0, sources, send, 0)
        landed[sh, me_t * 2 + me_c] = x16[sh, rows_of(me_t, me_c), :]

    def arrived(sh, g, count):
        block = landed.at[sh, pl.ds(0, count)]
        return pltpu.make_async_remote_copy(
            src_ref=block, dst_ref=block, send_sem=a_send.at[sh], recv_sem=a_recv.at[sh, g],
            device_id=at(me_t, me_y, 1 - me_c), device_id_type=MESH,
        )

    def pass_y(sh, g, h):
        block = grid_v.at[sh, g, me_y]
        return pltpu.make_async_remote_copy(
            src_ref=block, dst_ref=block, send_sem=y_send.at[sh, g, h], recv_sem=y_recv.at[sh, g, h],
            device_id=at(me_t, (y_up, y_down)[h], me_c), device_id_type=MESH,
        )

    def forward(sh, g, h):
        block = grid_v.at[sh, g, (y_down, y_up)[h], pl.ds(h * (HALF // 2), HALF // 2)]
        return pltpu.make_async_remote_copy(
            src_ref=block, dst_ref=block, send_sem=f_send.at[sh, g, h], recv_sem=f_recv.at[sh, g, h],
            device_id=at(me_t, (y_up, y_down)[h], me_c), device_id_type=MESH,
        )

    own_bunch = me_t // (n_theta // 4)

    def gather(sh, g):
        @pl.when(g == own_bunch)
        def _():
            arrived(sh, g, bunch - 1).wait_recv()

        @pl.when(g != own_bunch)
        def _():
            arrived(sh, g, bunch).wait_recv()

        spread[...] = landed[sh, pl.ds(g * bunch, bunch)].astype(jnp.float32).reshape(bunch * span, 128)
        for r in range(HALF):
            grid_v[sh, g, me_y, r] = jnp.concatenate(
                [spread[pl.ds(r * 4 + p, bunch, stride=span), :] for p in range(4)], axis=0
            ).astype(jnp.bfloat16)
        pass_y(sh, g, 0).start()
        pass_y(sh, g, 1).start()

    def relay(sh, g):
        for h in range(2):
            pass_y(sh, g, h).wait_recv()
            forward(sh, g, h).start()

    def far(sh, g):
        for h in range(2):
            forward(sh, g, h).wait_recv()

    lax.fori_loop(0, 2 * tiles, stage, 0)
    send_half(0)
    lax.fori_loop(2 * tiles, 4 * tiles, stage, 0)
    gather(0, 0)
    send_half(1)

    for r in reads[2:]:
        r.wait()
    index_v[0] = (cells_v[1] * QP + cells_v[0]) * 4
    index_v[1] = cells_v[2]
    to_smem = [pltpu.make_async_copy(index_v.at[n], dst, idx_sem.at[n]) for n, dst in enumerate((base_s, orient_s))]
    for copy in to_smem:
        copy.start()

    def product(sh, bunches, pair):
        count = bunches.stop - bunches.start
        right = jnp.concatenate(
            [grid_v[sh, bunches, :, 2 * pair + h].reshape(count * wide, 128) for h in range(2)], axis=1
        )
        left = table_v[sh, :, bunches.start * wide:bunches.stop * wide]
        return jnp.dot(left, right, preferred_element_type=jnp.float32)

    def first_part(pair, _):
        part_v[pair] = product(0, slice(0, 4), pair)
        return 0

    def second_part(pair, _):
        part_v[pair] += product(1, slice(0, 3), pair)
        return 0

    def step(n, _):
        @pl.when(n == 4)
        def _():
            lax.fori_loop(0, 8, table, 0)

        @pl.when(n < 8)
        def _():
            gather(n // 4, n % 4)

        @pl.when(n >= 3)
        def _():
            relay((n - 3) // 4, (n - 3) % 4)

        return 0

    lax.fori_loop(1, 11, step, 0)
    for g in range(4):
        far(0, g)
    lax.fori_loop(0, pairs, first_part, 0)
    for g in range(3):
        far(1, g)
    lax.fori_loop(0, pairs, second_part, 0)

    def share(n):
        return pltpu.make_async_remote_copy(
            src_ref=share_out.at[n], dst_ref=share_in.at[n], send_sem=s_send.at[n], recv_sem=s_recv.at[n],
            device_id=at(me_t, me_y, 1 - me_c), device_id_type=MESH,
        )

    def halo(n):
        t = (me_t + n_theta - 1 + 2 * me_c) % n_theta
        return pltpu.make_async_remote_copy(
            src_ref=halo_out.at[n], dst_ref=halo_in.at[1 - me_c], send_sem=h_send.at[n], recv_sem=h_recv.at[1 - me_c],
            device_id=at(t, me_y, (me_c + n) % 2), device_id_type=MESH,
        )

    edge_goes = jnp.logical_or(
        jnp.logical_and(me_c == 0, me_t > 0), jnp.logical_and(me_c == 1, me_t < n_theta - 1)
    )

    def put_taps(cell, b, value):
        for e, rows in enumerate((value, pltpu.roll(value, PSI - 1, 1))):
            taps[pl.ds(cell * (QP * 4) + 2 * b + e, QP, stride=4), :] = rows

    def put_cycle(r, value):
        turned = pltpu.roll(value, PSI - 1, 1)
        for cell, b in ((r + 1, 0), (r, 1)):
            for e, rows in enumerate((value, turned)):
                taps[pl.ds(cell * (QP * 4) + 2 * b + e, QP, stride=4), :] = rows

    def pair_at(n, c):
        return n + c * (pairs - 1 - 2 * n)

    def finish(n, _):
        pair = pair_at(n, me_c)

        both = product(1, slice(3, 4), pair) + part_v[pair]
        for h in range(2):
            share_out[n, h] = both[QP:, h * 128:(h + 1) * 128].astype(jnp.bfloat16)
        share(n).start()

        @pl.when(n == 0)
        def _():
            for i in range(2):
                rows = both[i * QP:(i + 1) * QP]
                halo_out[i] = jnp.where(me_c == 0, rows[:, :128], rows[:, 128:]).astype(jnp.bfloat16)

        @pl.when(jnp.logical_and(n == 0, edge_goes))
        def _():
            halo(0).start()
            halo(1).start()

        part_v[pair, :QP] = both[:QP]
        return 0

    def put_own(pair, _):
        for h in range(2):
            put_cycle(me_c * HALF + 2 * pair + h, part_v[pair, :QP, h * 128:(h + 1) * 128])
        return 0

    far(1, 3)
    lax.fori_loop(0, pairs, finish, 0)
    lax.fori_loop(0, pairs, put_own, 0)

    def take_share(n, _):
        share(n).wait_recv()
        for h in range(2):
            put_cycle((1 - me_c) * HALF + 2 * pair_at(n, 1 - me_c) + h, share_in[n, h].astype(jnp.float32))
        return 0

    lax.fori_loop(0, pairs, take_share, 0)

    def edge_in(slot):
        return pltpu.make_async_remote_copy(
            src_ref=halo_out.at[0], dst_ref=halo_in.at[slot], send_sem=h_send.at[0], recv_sem=h_recv.at[slot],
            device_id=at(me_t, me_y, 1 - me_c), device_id_type=MESH,
        )

    for slot, at_end in ((0, me_t == 0), (1, me_t == n_theta - 1)):
        @pl.when(jnp.logical_not(at_end))
        def _():
            edge_in(slot).wait_recv()

        @pl.when(at_end)
        def _():
            halo_in[slot] = jnp.zeros((QP, 128), jnp.bfloat16)

        put_taps(slot * RT, slot, halo_in[slot].astype(jnp.float32))

    for copy in to_smem:
        copy.wait()
    lane = lax.broadcasted_iota(jnp.int32, (8, 128), 1)

    count = count_s[0]

    def group(g, _):
        picked = jnp.zeros((8, 128), jnp.float32)
        for n in range(128):
            eight = taps[pl.ds(base_s[g, n], 8), :]
            tap = jnp.sum(jnp.where(lane == orient_s[g, n], eight, 0.0), axis=1, keepdims=True)
            picked = jnp.where(lane == n, tap, picked)
        weights = weight_v[:, pl.ds(pl.multiple_of(g * 128, 128), 128)]
        value = jnp.sum(picked * weights, axis=0, keepdims=True)
        out_ref[pl.ds(g, 1), :] = jnp.where(lane[0:1, :] + g * 128 < count, value, 0.0)
        return 0

    lax.fori_loop(0, groups, group, 0)

    @pl.when(edge_goes)
    def _():
        halo(0).wait_send()
        halo(1).wait_send()

    def drain(sh, _):
        arrived(sh, 0, others).wait_send()
        for g in range(4):
            for h in range(2):
                pass_y(sh, g, h).wait_send()
                forward(sh, g, h).wait_send()
        return 0

    lax.fori_loop(0, 2, drain, 0)

    def drain_share(n, _):
        share(n).wait_send()
        return 0

    lax.fori_loop(0, pairs, drain_share, 0)


def shards(
    alm, wig, slot_order, beam, phi_cell, theta_cell, orient_cell_index, tap_weight, sample_count
):
    n_theta, n_phi = lax.axis_size("theta"), lax.axis_size("phi")
    slots, _, ldeg = alm.shape
    m_all = slot_order.shape[0]
    tile = min(ldeg // 2, 4096)
    tiles = ldeg // tile
    n_y = n_phi // 2
    sources = 2 * n_theta
    block = sources
    pairs = HALF // 2
    groups = phi_cell.shape[0] // 128
    cells = [c.reshape(groups, 128) for c in (phi_cell, theta_cell, orient_cell_index)]
    anywhere = pl.BlockSpec(memory_space=pl.ANY)
    dma = pltpu.SemaphoreType.DMA
    f32, bf16, i32 = jnp.float32, jnp.bfloat16, jnp.int32
    value = pl.pallas_call(
        functools.partial(kernel, n_theta, n_phi, slots, ldeg, tile, m_all, groups),
        out_shape=jax.ShapeDtypeStruct((groups, 128), f32),
        in_specs=[anywhere] * 9,
        out_specs=pl.BlockSpec(memory_space=pltpu.VMEM),
        scratch_shapes=[
            pltpu.VMEM((slots * tiles, wig.shape[1], tile), bf16),
            pltpu.VMEM(beam.shape, bf16),
            pltpu.VMEM((tiles, 128, tile), bf16),
            pltpu.VMEM(alm.shape, bf16),
            pltpu.VMEM((slots, 2, 16, ldeg), bf16),
            pltpu.VMEM((1, m_all), i32),
            pltpu.VMEM((3, groups, 128), i32),
            pltpu.VMEM(tap_weight.shape, f32),
            pltpu.VMEM((256, 256), bf16),
            pltpu.VMEM((2, n_theta * RT, 256), f32),
            pltpu.VMEM((n_theta * RT * 4, 128), f32),
            pltpu.VMEM((2, n_theta * RT * 4, 128), bf16),
            pltpu.VMEM((2, sources, HALF * 4, 128), bf16),
            pltpu.VMEM((sources // 4 * HALF * 4, 128), f32),
            pltpu.VMEM((2, 4, n_y, HALF, block, 128), bf16),
            pltpu.VMEM((2, 2 * QP, 4 * n_y * block), bf16),
            pltpu.VMEM((pairs, 2 * QP, 256), f32),
            pltpu.VMEM((pairs, 2, QP, 128), bf16),
            pltpu.VMEM((pairs, 2, QP, 128), bf16),
            pltpu.VMEM((2, QP, 128), bf16),
            pltpu.VMEM((2, QP, 128), bf16),
            pltpu.VMEM(((RT + 1) * QP * 4 + 8, 128), f32),
            pltpu.VMEM((2, groups, 128), i32),
            pltpu.SMEM((groups, 128), i32),
            pltpu.SMEM((groups, 128), i32),
            pltpu.SMEM((1,), i32),
            dma((slots * tiles,)), dma((tiles,)), dma((7,)), dma((2,)),
            dma((2,)), dma((2, 4)),
            dma((2, 4, 2)), dma((2, 4, 2)),
            dma((2, 4, 2)), dma((2, 4, 2)),
            dma((pairs,)), dma((pairs,)),
            dma((2,)), dma((2,)),
        ],
        compiler_params=pltpu.CompilerParams(
            collective_id=0, has_side_effects=True, vmem_limit_bytes=58 << 20
        ),
        name="convolve",
    )(wig, alm, beam, slot_order.reshape(1, -1), *cells, tap_weight, sample_count)
    return value.reshape(-1)


def solution(mesh):
    return jax.shard_map(
        shards,
        mesh=mesh,
        in_specs=(
            P(("theta", "phi"), None, None),
            P(("theta", "phi"), None, None),
            P(),
            P(),
            P(("theta", "phi")),
            P(("theta", "phi")),
            P(("theta", "phi")),
            P(None, ("theta", "phi")),
            P(("theta", "phi")),
        ),
        out_specs=P(("theta", "phi")),
        check_vma=False,
    )
```

```python
import functools
import math

import jax
import jax.numpy as jnp
from jax import lax
from jax.experimental import pallas as pl
from jax.experimental.pallas import tpu as pltpu
from jax.sharding import PartitionSpec as P

PSI = 128
PD = 192
RT = 16
QP = 208
HALF = RT // 2
BUNCHES = 2
LAG = 3
MESH = pl.DeviceIdType.MESH
NT = (((1,), (1,)), ((), ()))


def slot_m(order, half, m_all):
    stride = max(half // m_all, 1)
    m = lax.shift_right_logical(order * half, m_all.bit_length() - 1)
    if stride > 1:
        m = m + (7 * order) % stride
    return m


def turn_cos(phase, total):
    x = (jnp.abs(phase - total / 2) - total / 4) * (2.0 * math.pi / total)
    x2 = x * x
    p = jnp.float32(-1.0 / math.factorial(11))
    for n in (9, 7, 5, 3, 1):
        p = p * x2 + jnp.float32((-1) ** (n // 2) / math.factorial(n))
    return p * x


def wrap(value, total):
    return value - jnp.floor((value + 0.5) * jnp.float32(1.0 / total)) * total


def psi_rows():
    k_at = lax.broadcasted_iota(jnp.int32, (128, 128), 0)
    p_at = lax.broadcasted_iota(jnp.int32, (128, 128), 1)
    turn = ((k_at * p_at) & (PSI - 1)).astype(jnp.float32)
    scale = 1.0 / math.sqrt(2 * 128)
    psi0 = turn_cos(turn, PSI) * scale
    psi1 = -turn_cos(wrap(turn + 0.75 * PSI, PSI), PSI) * scale
    return psi0.astype(jnp.bfloat16), psi1.astype(jnp.bfloat16), (-psi0).astype(jnp.bfloat16)


def kernel(
    n_theta, n_phi, slots, ldeg, tile, m_all, groups,
    wig_hbm, alm_hbm, beam_hbm, order_hbm, phi_hbm, theta_hbm, orient_hbm, weight_hbm, count_hbm, out_ref,
    wig_v, beam_v, beam_t, alm_v, sky_v, order_v, cells_v, weight_v, psi_v, sums, x32, x16, landed, spread, grid_v,
    table_v, part_v, share_out, share_in, halo_out, halo_in, taps, index_v,
    base_s, orient_s, count_s, wig_sem, beam_sem, in_sem, idx_sem, a_send, a_recv, y_send, y_recv, f_send, f_recv, s_send, s_recv, h_send, h_recv,
):
    me_t = lax.axis_index("theta")
    me_p = lax.axis_index("phi")
    me_y, me_c = me_p // 2, me_p % 2
    n_y = n_phi // 2
    total = PD * n_phi
    tiles = ldeg // tile
    sources = 2 * n_theta
    bunch = sources // BUNCHES
    span = HALF * 4
    per_block = 4 * bunch
    wide = n_y * per_block
    pairs = HALF // 2
    y_up, y_down, y_far = (me_y + 1) % n_y, (me_y + n_y - 1) % n_y, (me_y + 2) % n_y

    def at(t, y, c):
        return (t, y * 2 + c)

    reads = [
        pltpu.make_async_copy(src, dst, in_sem.at[n])
        for n, (src, dst) in enumerate(
            (
                (alm_hbm, alm_v), (order_hbm, order_v), (count_hbm, count_s), (phi_hbm, cells_v.at[0]),
                (theta_hbm, cells_v.at[1]), (orient_hbm, cells_v.at[2]), (weight_hbm, weight_v),
            )
        )
    ]

    def place(n):
        sh, i, s2 = n // (2 * tiles), n // 2 % tiles, n % 2
        return sh * 2 + s2, i

    def wig_copy(n):
        s, i = place(n)
        return pltpu.make_async_copy(
            wig_hbm.at[s, :, pl.ds(pl.multiple_of(i * tile, 128), tile)], wig_v.at[n], wig_sem.at[n]
        )

    def beam_copy(i):
        part = pl.ds(pl.multiple_of(i * tile, 128), tile)
        return pltpu.make_async_copy(beam_hbm.at[part, :], beam_v.at[part, :], beam_sem.at[i])

    for r in reads[:2]:
        r.start()
    for i in range(tiles):
        beam_copy(i).start()

    def wig_start(n, _):
        wig_copy(n).start()
        return 0

    lax.fori_loop(0, 2 * tiles, wig_start, 0)
    for r in reads[2:]:
        r.start()

    def target(n):
        m = n + 5 * sources // 8
        return (me_t + m // 2) & (n_theta - 1), (me_c + m) & 1

    barrier = pltpu.get_barrier_semaphore()

    def greet(n, _):
        t, c = target(n)

        @pl.when(n != alone)
        def _():
            pl.semaphore_signal(barrier, inc=1, device_id=at(t, me_y, c), device_id_type=MESH)

        return 0

    others = sources - 1
    alone = sources - 5 * sources // 8
    lax.fori_loop(0, sources, greet, 0)
    for y in (y_up, y_down):
        pl.semaphore_signal(barrier, inc=1, device_id=at(me_t, y, me_c), device_id_type=MESH)

    psi0, psi1, psi2 = psi_rows()
    psi_v[:128, :128] = psi0
    psi_v[:128, 128:] = psi1
    psi_v[128:, :128] = psi1
    psi_v[128:, 128:] = psi2
    for r in reads[:2]:
        r.wait()

    m_row = slot_m(order_v[...], total // 2, m_all)
    slot_lane = lax.broadcasted_iota(jnp.int32, (1, m_all), 1)
    eye = (
        lax.broadcasted_iota(jnp.int32, (128, 128), 0) == lax.broadcasted_iota(jnp.int32, (128, 128), 1)
    ).astype(jnp.bfloat16)

    m_hi = lax.shift_right_logical(m_row, 4).astype(jnp.float32)
    m_lo = (m_row & 15).astype(jnp.float32)
    split = jnp.concatenate([m_hi, m_lo, jnp.zeros((6, m_all), jnp.float32)], axis=0).astype(jnp.bfloat16)
    col = lax.broadcasted_iota(jnp.int32, (1, wide), 1)
    part = col % per_block // bunch
    source = col % bunch
    slot_col = (source // 2 * n_phi + col // per_block * 2 + source % 2) * slots + part // 2
    n_at = lax.broadcasted_iota(jnp.int32, (m_all, wide), 0)
    part_at = (part % 2).astype(jnp.float32)
    row = lax.broadcasted_iota(jnp.int32, (2 * QP, 1), 0)
    sibling = me_y * 2 + 1 - me_c
    q_at = jnp.where(row < QP, row + me_p * PD, row - QP + sibling * PD) - 1 + total
    q_at = q_at.astype(jnp.float32)

    def table(n, _):
        sh, g = n // BUNCHES, n % BUNCHES
        first = g * (n_theta // BUNCHES) * n_phi * slots + sh * 2
        pick = (n_at == slot_col + first).astype(jnp.bfloat16)
        moved = jnp.dot(split, pick, preferred_element_type=jnp.float32)
        m_col = moved[0:1, :] * 16.0 + moved[1:2, :]
        phase = wrap(m_col * q_at + (1.0 - part_at * 0.25) * total, total)
        table_v[sh, :, pl.ds(pl.multiple_of(g * wide, wide), wide)] = (
            turn_cos(phase, total) * (1.0 / math.sqrt(m_all))
        ).astype(jnp.bfloat16)
        return 0

    def turn_beam(i, _):
        beam_copy(i).wait()
        beam_t[i] = lax.dot_general(
            eye, beam_v[pl.ds(pl.multiple_of(i * tile, 128), tile), :], NT, preferred_element_type=jnp.float32
        ).astype(jnp.bfloat16)
        return 0

    def mask_sky(s, _):
        mine = slot_lane == (me_t * n_phi + me_p) * slots + s
        m_own = jnp.sum(jnp.where(mine, m_row, 0).astype(jnp.float32), axis=1, keepdims=True)
        degree = lax.broadcasted_iota(jnp.int32, (2, ldeg), 1).astype(jnp.float32)
        sky = jnp.where(degree >= m_own, alm_v[s].astype(jnp.float32), 0.0)
        for c in range(2):
            sky_v[s, c] = jnp.broadcast_to(sky[c:c + 1, :], (16, ldeg)).astype(jnp.bfloat16)
        return 0

    lax.fori_loop(0, 2, mask_sky, 0)
    lax.fori_loop(0, tiles, turn_beam, 0)

    def stage(n, _):
        s, i = place(n)
        part = beam_t[i].reshape(8, 16, tile)
        span_i = pl.ds(pl.multiple_of(i * tile, 128), tile)
        weighted = jnp.concatenate(
            [(part * sky_v[s, c, :, span_i][None]).reshape(128, tile) for c in range(2)], axis=0
        )
        wig_copy(n).wait()

        @pl.when(n < (slots - 2) * tiles)
        def _():
            wig_copy(n + 2 * tiles).start()

        term = lax.dot_general(wig_v[n], weighted, NT, preferred_element_type=jnp.float32)

        @pl.when(i == 0)
        def _():
            sums[n % 2] = term

        @pl.when(i > 0)
        def _():
            sums[n % 2] += term

        return 0

    def rows_of(t, c):
        return pl.ds(pl.multiple_of((t * 2 + c) * span, 16), span)

    def send_half(sh):
        def to_psi(s2, _):
            x = jnp.dot(sums[s2].astype(jnp.bfloat16), psi_v[...], preferred_element_type=jnp.float32)
            for c in range(2):
                x32[pl.ds(2 * s2 + c, n_theta * RT, stride=4), :] = x[:, c * 128:(c + 1) * 128]
            return 0

        lax.fori_loop(0, 2, to_psi, 0)

        x16[sh] = x32[...].astype(jnp.bfloat16)

        if sh == 0:
            pl.semaphore_wait(barrier, others + 2)

        def send(n, _):
            t, c = target(n)

            @pl.when(n != alone)
            def _():
                pltpu.make_async_remote_copy(
                    src_ref=x16.at[sh, rows_of(t, c), :], dst_ref=landed.at[sh, me_t * 2 + me_c],
                    send_sem=a_send.at[sh], recv_sem=a_recv.at[sh, me_t // (n_theta // BUNCHES)],
                    device_id=at(t, me_y, c), device_id_type=MESH,
                ).start()

            return 0

        lax.fori_loop(0, sources, send, 0)
        landed[sh, me_t * 2 + me_c] = x16[sh, rows_of(me_t, me_c), :]

    def arrived(sh, g, count):
        block = landed.at[sh, pl.ds(0, count)]
        return pltpu.make_async_remote_copy(
            src_ref=block, dst_ref=block, send_sem=a_send.at[sh], recv_sem=a_recv.at[sh, g],
            device_id=at(me_t, me_y, 1 - me_c), device_id_type=MESH,
        )

    def pass_y(sh, g, h):
        block = grid_v.at[sh, g, me_y]
        return pltpu.make_async_remote_copy(
            src_ref=block, dst_ref=block, send_sem=y_send.at[sh, g, h], recv_sem=y_recv.at[sh, g, h],
            device_id=at(me_t, (y_up, y_down)[h], me_c), device_id_type=MESH,
        )

    def forward(sh, g, h):
        block = grid_v.at[sh, g, (y_down, y_up)[h], pl.ds(h * (HALF // 2), HALF // 2)]
        return pltpu.make_async_remote_copy(
            src_ref=block, dst_ref=block, send_sem=f_send.at[sh, g, h], recv_sem=f_recv.at[sh, g, h],
            device_id=at(me_t, (y_up, y_down)[h], me_c), device_id_type=MESH,
        )

    own_bunch = me_t // (n_theta // BUNCHES)

    def gather(sh, g):
        @pl.when(g == own_bunch)
        def _():
            arrived(sh, g, bunch - 1).wait_recv()

        @pl.when(g != own_bunch)
        def _():
            arrived(sh, g, bunch).wait_recv()

        spread[...] = landed[sh, pl.ds(g * bunch, bunch)].astype(jnp.float32).reshape(bunch * span, 128)
        for r in range(HALF):
            grid_v[sh, g, me_y, r] = jnp.concatenate(
                [spread[pl.ds(r * 4 + p, bunch, stride=span), :] for p in range(4)], axis=0
            ).astype(jnp.bfloat16)
        pass_y(sh, g, 0).start()
        pass_y(sh, g, 1).start()

    def relay(sh, g):
        for h in range(2):
            pass_y(sh, g, h).wait_recv()
            forward(sh, g, h).start()

    def far(sh, g):
        for h in range(2):
            forward(sh, g, h).wait_recv()

    lax.fori_loop(0, 2 * tiles, stage, 0)
    send_half(0)
    lax.fori_loop(2, slots, mask_sky, 0)
    lax.fori_loop(2 * tiles, 4 * tiles, stage, 0)
    gather(0, 0)
    send_half(1)

    for r in reads[2:]:
        r.wait()
    index_v[0] = (cells_v[1] * QP + cells_v[0]) * 4
    index_v[1] = cells_v[2]
    to_smem = [pltpu.make_async_copy(index_v.at[n], dst, idx_sem.at[n]) for n, dst in enumerate((base_s, orient_s))]
    for copy in to_smem:
        copy.start()

    def product(sh, bunches, pair):
        count = bunches.stop - bunches.start
        right = jnp.concatenate(
            [grid_v[sh, bunches, :, 2 * pair + h].reshape(count * wide, 128) for h in range(2)], axis=1
        )
        left = table_v[sh, :, bunches.start * wide:bunches.stop * wide]
        return jnp.dot(left, right, preferred_element_type=jnp.float32)

    def first_part(pair, _):
        part_v[pair] = product(0, slice(0, BUNCHES), pair)
        return 0

    def second_part(pair, _):
        part_v[pair] += product(1, slice(0, BUNCHES - 1), pair)
        return 0

    def step(n, _):
        @pl.when(n == BUNCHES)
        def _():
            lax.fori_loop(0, 2 * BUNCHES, table, 0)

        @pl.when(n < 2 * BUNCHES)
        def _():
            gather(n // BUNCHES, n % BUNCHES)

        @pl.when(n >= LAG)
        def _():
            relay((n - LAG) // BUNCHES, (n - LAG) % BUNCHES)

        return 0

    lax.fori_loop(1, 2 * BUNCHES + LAG, step, 0)
    for g in range(BUNCHES):
        far(0, g)
    lax.fori_loop(0, pairs, first_part, 0)
    for g in range(BUNCHES - 1):
        far(1, g)
    lax.fori_loop(0, pairs, second_part, 0)

    def share(n):
        return pltpu.make_async_remote_copy(
            src_ref=share_out.at[n], dst_ref=share_in.at[n], send_sem=s_send.at[n], recv_sem=s_recv.at[n],
            device_id=at(me_t, me_y, 1 - me_c), device_id_type=MESH,
        )

    def halo(n):
        t = (me_t + n_theta - 1 + 2 * me_c) % n_theta
        return pltpu.make_async_remote_copy(
            src_ref=halo_out.at[n], dst_ref=halo_in.at[1 - me_c], send_sem=h_send.at[n], recv_sem=h_recv.at[1 - me_c],
            device_id=at(t, me_y, (me_c + n) % 2), device_id_type=MESH,
        )

    edge_goes = jnp.logical_or(
        jnp.logical_and(me_c == 0, me_t > 0), jnp.logical_and(me_c == 1, me_t < n_theta - 1)
    )

    def put_taps(cell, b, value):
        for e, rows in enumerate((value, pltpu.roll(value, PSI - 1, 1))):
            taps[pl.ds(cell * (QP * 4) + 2 * b + e, QP, stride=4), :] = rows

    def put_cycle(r, value):
        turned = pltpu.roll(value, PSI - 1, 1)
        for cell, b in ((r + 1, 0), (r, 1)):
            for e, rows in enumerate((value, turned)):
                taps[pl.ds(cell * (QP * 4) + 2 * b + e, QP, stride=4), :] = rows

    def pair_at(n, c):
        return n + c * (pairs - 1 - 2 * n)

    def finish(n, _):
        pair = pair_at(n, me_c)

        both = product(1, slice(BUNCHES - 1, BUNCHES), pair) + part_v[pair]
        for h in range(2):
            share_out[n, h] = both[QP:, h * 128:(h + 1) * 128].astype(jnp.bfloat16)
        share(n).start()

        @pl.when(n == 0)
        def _():
            for i in range(2):
                rows = both[i * QP:(i + 1) * QP]
                halo_out[i] = jnp.where(me_c == 0, rows[:, :128], rows[:, 128:]).astype(jnp.bfloat16)

        @pl.when(jnp.logical_and(n == 0, edge_goes))
        def _():
            halo(0).start()
            halo(1).start()

        part_v[pair, :QP] = both[:QP]
        return 0

    def put_own(pair, _):
        for h in range(2):
            put_cycle(me_c * HALF + 2 * pair + h, part_v[pair, :QP, h * 128:(h + 1) * 128])
        return 0

    far(1, BUNCHES - 1)
    lax.fori_loop(0, pairs, finish, 0)
    lax.fori_loop(0, pairs, put_own, 0)

    def take_share(n, _):
        share(n).wait_recv()
        for h in range(2):
            put_cycle((1 - me_c) * HALF + 2 * pair_at(n, 1 - me_c) + h, share_in[n, h].astype(jnp.float32))
        return 0

    lax.fori_loop(0, pairs, take_share, 0)

    def edge_in(slot):
        return pltpu.make_async_remote_copy(
            src_ref=halo_out.at[0], dst_ref=halo_in.at[slot], send_sem=h_send.at[0], recv_sem=h_recv.at[slot],
            device_id=at(me_t, me_y, 1 - me_c), device_id_type=MESH,
        )

    for slot, at_end in ((0, me_t == 0), (1, me_t == n_theta - 1)):
        @pl.when(jnp.logical_not(at_end))
        def _():
            edge_in(slot).wait_recv()

        @pl.when(at_end)
        def _():
            halo_in[slot] = jnp.zeros((QP, 128), jnp.bfloat16)

        put_taps(slot * RT, slot, halo_in[slot].astype(jnp.float32))

    for copy in to_smem:
        copy.wait()
    lane = lax.broadcasted_iota(jnp.int32, (8, 128), 1)

    count = count_s[0]

    def group(g, _):
        picked = jnp.zeros((8, 128), jnp.float32)
        for n in range(128):
            eight = taps[pl.ds(base_s[g, n], 8), :]
            tap = jnp.sum(jnp.where(lane == orient_s[g, n], eight, 0.0), axis=1, keepdims=True)
            picked = jnp.where(lane == n, tap, picked)
        weights = weight_v[:, pl.ds(pl.multiple_of(g * 128, 128), 128)]
        value = jnp.sum(picked * weights, axis=0, keepdims=True)
        out_ref[pl.ds(g, 1), :] = jnp.where(lane[0:1, :] + g * 128 < count, value, 0.0)
        return 0

    lax.fori_loop(0, groups, group, 0)

    @pl.when(edge_goes)
    def _():
        halo(0).wait_send()
        halo(1).wait_send()

    def drain(sh, _):
        arrived(sh, 0, others).wait_send()
        for g in range(BUNCHES):
            for h in range(2):
                pass_y(sh, g, h).wait_send()
                forward(sh, g, h).wait_send()
        return 0

    lax.fori_loop(0, 2, drain, 0)

    def drain_share(n, _):
        share(n).wait_send()
        return 0

    lax.fori_loop(0, pairs, drain_share, 0)


def shards(
    alm, wig, slot_order, beam, phi_cell, theta_cell, orient_cell_index, tap_weight, sample_count
):
    n_theta, n_phi = lax.axis_size("theta"), lax.axis_size("phi")
    slots, _, ldeg = alm.shape
    m_all = slot_order.shape[0]
    tile = min(ldeg // 2, 4096)
    tiles = ldeg // tile
    n_y = n_phi // 2
    sources = 2 * n_theta
    block = 4 * sources // BUNCHES
    pairs = HALF // 2
    groups = phi_cell.shape[0] // 128
    cells = [c.reshape(groups, 128) for c in (phi_cell, theta_cell, orient_cell_index)]
    anywhere = pl.BlockSpec(memory_space=pl.ANY)
    dma = pltpu.SemaphoreType.DMA
    f32, bf16, i32 = jnp.float32, jnp.bfloat16, jnp.int32
    value = pl.pallas_call(
        functools.partial(kernel, n_theta, n_phi, slots, ldeg, tile, m_all, groups),
        out_shape=jax.ShapeDtypeStruct((groups, 128), f32),
        in_specs=[anywhere] * 9,
        out_specs=pl.BlockSpec(memory_space=pltpu.VMEM),
        scratch_shapes=[
            pltpu.VMEM((slots * tiles, wig.shape[1], tile), bf16),
            pltpu.VMEM(beam.shape, bf16),
            pltpu.VMEM((tiles, 128, tile), bf16),
            pltpu.VMEM(alm.shape, bf16),
            pltpu.VMEM((slots, 2, 16, ldeg), bf16),
            pltpu.VMEM((1, m_all), i32),
            pltpu.VMEM((3, groups, 128), i32),
            pltpu.VMEM(tap_weight.shape, f32),
            pltpu.VMEM((256, 256), bf16),
            pltpu.VMEM((2, n_theta * RT, 256), f32),
            pltpu.VMEM((n_theta * RT * 4, 128), f32),
            pltpu.VMEM((2, n_theta * RT * 4, 128), bf16),
            pltpu.VMEM((2, sources, HALF * 4, 128), bf16),
            pltpu.VMEM((sources // BUNCHES * HALF * 4, 128), f32),
            pltpu.VMEM((2, BUNCHES, n_y, HALF, block, 128), bf16),
            pltpu.VMEM((2, 2 * QP, BUNCHES * n_y * block), bf16),
            pltpu.VMEM((pairs, 2 * QP, 256), f32),
            pltpu.VMEM((pairs, 2, QP, 128), bf16),
            pltpu.VMEM((pairs, 2, QP, 128), bf16),
            pltpu.VMEM((2, QP, 128), bf16),
            pltpu.VMEM((2, QP, 128), bf16),
            pltpu.VMEM(((RT + 1) * QP * 4 + 8, 128), f32),
            pltpu.VMEM((2, groups, 128), i32),
            pltpu.SMEM((groups, 128), i32),
            pltpu.SMEM((groups, 128), i32),
            pltpu.SMEM((1,), i32),
            dma((slots * tiles,)), dma((tiles,)), dma((7,)), dma((2,)),
            dma((2,)), dma((2, BUNCHES)),
            dma((2, BUNCHES, 2)), dma((2, BUNCHES, 2)),
            dma((2, BUNCHES, 2)), dma((2, BUNCHES, 2)),
            dma((pairs,)), dma((pairs,)),
            dma((2,)), dma((2,)),
        ],
        compiler_params=pltpu.CompilerParams(
            collective_id=0, has_side_effects=True, vmem_limit_bytes=58 << 20
        ),
        name="convolve",
    )(wig, alm, beam, slot_order.reshape(1, -1), *cells, tap_weight, sample_count)
    return value.reshape(-1)


def solution(mesh):
    return jax.shard_map(
        shards,
        mesh=mesh,
        in_specs=(
            P(("theta", "phi"), None, None),
            P(("theta", "phi"), None, None),
            P(),
            P(),
            P(("theta", "phi")),
            P(("theta", "phi")),
            P(("theta", "phi")),
            P(None, ("theta", "phi")),
            P(("theta", "phi")),
        ),
        out_specs=P(("theta", "phi")),
        check_vma=False,
    )
```

```python
import functools
import math

import jax
import jax.numpy as jnp
from jax import lax
from jax.experimental import pallas as pl
from jax.experimental.pallas import tpu as pltpu
from jax.sharding import PartitionSpec as P

PSI = 128
PD = 192
RT = 16
QP = 208
HALF = RT // 2
BUNCHES = 2
LAG = 3
MESH = pl.DeviceIdType.MESH
NT = (((1,), (1,)), ((), ()))


def slot_m(order, half, m_all):
    stride = max(half // m_all, 1)
    m = lax.shift_right_logical(order * half, m_all.bit_length() - 1)
    if stride > 1:
        m = m + (7 * order) % stride
    return m


def turn_cos(phase, total):
    x = (jnp.abs(phase - total / 2) - total / 4) * (2.0 * math.pi / total)
    x2 = x * x
    p = jnp.float32(-1.0 / math.factorial(11))
    for n in (9, 7, 5, 3, 1):
        p = p * x2 + jnp.float32((-1) ** (n // 2) / math.factorial(n))
    return p * x


def wrap(value, total):
    return value - jnp.floor((value + 0.5) * jnp.float32(1.0 / total)) * total


def psi_rows():
    k_at = lax.broadcasted_iota(jnp.int32, (128, 128), 0)
    p_at = lax.broadcasted_iota(jnp.int32, (128, 128), 1)
    turn = ((k_at * p_at) & (PSI - 1)).astype(jnp.float32)
    scale = 1.0 / math.sqrt(2 * 128)
    psi0 = turn_cos(turn, PSI) * scale
    psi1 = -turn_cos(wrap(turn + 0.75 * PSI, PSI), PSI) * scale
    return psi0.astype(jnp.bfloat16), psi1.astype(jnp.bfloat16), (-psi0).astype(jnp.bfloat16)


def kernel(
    n_theta, n_phi, slots, ldeg, tile, m_all, groups,
    wig_hbm, alm_hbm, beam_hbm, order_hbm, phi_hbm, theta_hbm, orient_hbm, weight_hbm, count_hbm, out_ref,
    wig_v, beam_v, beam_t, alm_v, sky_v, order_v, cells_v, weight_v, psi_v, sums, x32, x16, landed, spread, grid_v,
    table_v, part_v, share_out, share_in, halo_out, halo_in, taps, index_v,
    base_s, orient_s, count_s, wig_sem, beam_sem, in_sem, idx_sem, a_send, a_recv, y_send, y_recv, f_send, f_recv, s_send, s_recv, h_send, h_recv,
):
    me_t = lax.axis_index("theta")
    me_p = lax.axis_index("phi")
    me_y, me_c = me_p // 2, me_p % 2
    n_y = n_phi // 2
    total = PD * n_phi
    tiles = ldeg // tile
    sources = 2 * n_theta
    bunch = sources // BUNCHES
    span = HALF * 4
    per_block = 4 * bunch
    wide = n_y * per_block
    pairs = HALF // 2
    y_up, y_down, y_far = (me_y + 1) % n_y, (me_y + n_y - 1) % n_y, (me_y + 2) % n_y

    def at(t, y, c):
        return (t, y * 2 + c)

    reads = [
        pltpu.make_async_copy(src, dst, in_sem.at[n])
        for n, (src, dst) in enumerate(
            (
                (alm_hbm, alm_v), (order_hbm, order_v), (count_hbm, count_s), (phi_hbm, cells_v.at[0]),
                (theta_hbm, cells_v.at[1]), (orient_hbm, cells_v.at[2]), (weight_hbm, weight_v),
            )
        )
    ]

    def place(n):
        sh, i, s2 = n // (2 * tiles), n // 2 % tiles, n % 2
        return sh * 2 + s2, i

    def wig_copy(n):
        s, i = place(n)
        return pltpu.make_async_copy(
            wig_hbm.at[s, :, pl.ds(pl.multiple_of(i * tile, 128), tile)], wig_v.at[n], wig_sem.at[n]
        )

    def beam_copy(i):
        part = pl.ds(pl.multiple_of(i * tile, 128), tile)
        return pltpu.make_async_copy(beam_hbm.at[part, :], beam_v.at[part, :], beam_sem.at[i])

    for r in reads[:2]:
        r.start()
    for i in range(tiles):
        beam_copy(i).start()

    def wig_start(n, _):
        wig_copy(n).start()
        return 0

    lax.fori_loop(0, 2 * tiles, wig_start, 0)
    for r in reads[2:]:
        r.start()

    def target(n):
        m = n + 5 * sources // 8
        return (me_t + m // 2) & (n_theta - 1), (me_c + m) & 1

    barrier = pltpu.get_barrier_semaphore()

    def greet(n, _):
        t, c = target(n)

        @pl.when(n != alone)
        def _():
            pl.semaphore_signal(barrier, inc=1, device_id=at(t, me_y, c), device_id_type=MESH)

        return 0

    others = sources - 1
    alone = sources - 5 * sources // 8
    lax.fori_loop(0, sources, greet, 0)
    for y in (y_up, y_down):
        pl.semaphore_signal(barrier, inc=1, device_id=at(me_t, y, me_c), device_id_type=MESH)

    psi0, psi1, psi2 = psi_rows()
    psi_v[:128, :128] = psi0
    psi_v[:128, 128:] = psi1
    psi_v[128:, :128] = psi1
    psi_v[128:, 128:] = psi2
    for r in reads[:2]:
        r.wait()

    m_row = slot_m(order_v[...], total // 2, m_all)
    slot_lane = lax.broadcasted_iota(jnp.int32, (1, m_all), 1)
    eye = (
        lax.broadcasted_iota(jnp.int32, (128, 128), 0) == lax.broadcasted_iota(jnp.int32, (128, 128), 1)
    ).astype(jnp.bfloat16)

    m_hi = lax.shift_right_logical(m_row, 4).astype(jnp.float32)
    m_lo = (m_row & 15).astype(jnp.float32)
    split = jnp.concatenate([m_hi, m_lo, jnp.zeros((6, m_all), jnp.float32)], axis=0).astype(jnp.bfloat16)
    col = lax.broadcasted_iota(jnp.int32, (1, wide), 1)
    part = col % per_block // bunch
    source = col % bunch
    slot_col = (source // 2 * n_phi + col // per_block * 2 + source % 2) * slots + part // 2
    n_at = lax.broadcasted_iota(jnp.int32, (m_all, wide), 0)
    part_at = (part % 2).astype(jnp.float32)
    row = lax.broadcasted_iota(jnp.int32, (2 * QP, 1), 0)
    sibling = me_y * 2 + 1 - me_c
    q_at = jnp.where(row < QP, row + me_p * PD, row - QP + sibling * PD) - 1 + total
    q_at = q_at.astype(jnp.float32)

    def table(n, _):
        sh, g = n // BUNCHES, n % BUNCHES
        first = g * (n_theta // BUNCHES) * n_phi * slots + sh * 2
        pick = (n_at == slot_col + first).astype(jnp.bfloat16)
        moved = jnp.dot(split, pick, preferred_element_type=jnp.float32)
        m_col = moved[0:1, :] * 16.0 + moved[1:2, :]
        phase = wrap(m_col * q_at + (1.0 - part_at * 0.25) * total, total)
        table_v[sh, :, pl.ds(pl.multiple_of(g * wide, wide), wide)] = (
            turn_cos(phase, total) * (1.0 / math.sqrt(m_all))
        ).astype(jnp.bfloat16)
        return 0

    def turn_beam(i, _):
        beam_copy(i).wait()
        beam_t[i] = lax.dot_general(
            eye, beam_v[pl.ds(pl.multiple_of(i * tile, 128), tile), :], NT, preferred_element_type=jnp.float32
        ).astype(jnp.bfloat16)
        return 0

    def mask_sky(s, _):
        mine = slot_lane == (me_t * n_phi + me_p) * slots + s
        m_own = jnp.sum(jnp.where(mine, m_row, 0).astype(jnp.float32), axis=1, keepdims=True)
        degree = lax.broadcasted_iota(jnp.int32, (2, ldeg), 1).astype(jnp.float32)
        sky = jnp.where(degree >= m_own, alm_v[s].astype(jnp.float32), 0.0)
        for c in range(2):
            sky_v[s, c] = jnp.broadcast_to(sky[c:c + 1, :], (16, ldeg)).astype(jnp.bfloat16)
        return 0

    lax.fori_loop(0, 2, mask_sky, 0)
    lax.fori_loop(0, tiles, turn_beam, 0)

    def stage(n, _):
        s, i = place(n)
        part = beam_t[i].reshape(8, 16, tile)
        span_i = pl.ds(pl.multiple_of(i * tile, 128), tile)
        weighted = jnp.concatenate(
            [(part * sky_v[s, c, :, span_i][None]).reshape(128, tile) for c in range(2)], axis=0
        )
        wig_copy(n).wait()

        @pl.when(n < (slots - 2) * tiles)
        def _():
            wig_copy(n + 2 * tiles).start()

        term = lax.dot_general(wig_v[n], weighted, NT, preferred_element_type=jnp.float32)

        @pl.when(i == 0)
        def _():
            sums[n % 2] = term

        @pl.when(i > 0)
        def _():
            sums[n % 2] += term

        return 0

    def rows_of(t, c):
        return pl.ds(pl.multiple_of((t * 2 + c) * span, 16), span)

    def send_half(sh):
        def to_psi(s2, _):
            x = jnp.dot(sums[s2].astype(jnp.bfloat16), psi_v[...], preferred_element_type=jnp.float32)
            for c in range(2):
                x32[pl.ds(2 * s2 + c, n_theta * RT, stride=4), :] = x[:, c * 128:(c + 1) * 128]
            return 0

        lax.fori_loop(0, 2, to_psi, 0)

        x16[sh] = x32[:n_theta * RT * 4, :].astype(jnp.bfloat16)

        if sh == 0:
            pl.semaphore_wait(barrier, others + 2)

        def send(n, _):
            t, c = target(n)

            @pl.when(n != alone)
            def _():
                pltpu.make_async_remote_copy(
                    src_ref=x16.at[sh, rows_of(t, c), :], dst_ref=landed.at[sh, me_t * 2 + me_c],
                    send_sem=a_send.at[sh], recv_sem=a_recv.at[sh, me_t // (n_theta // BUNCHES)],
                    device_id=at(t, me_y, c), device_id_type=MESH,
                ).start()

            return 0

        lax.fori_loop(0, sources, send, 0)
        landed[sh, me_t * 2 + me_c] = x16[sh, rows_of(me_t, me_c), :]

    def arrived(sh, g, count):
        block = landed.at[sh, pl.ds(0, count)]
        return pltpu.make_async_remote_copy(
            src_ref=block, dst_ref=block, send_sem=a_send.at[sh], recv_sem=a_recv.at[sh, g],
            device_id=at(me_t, me_y, 1 - me_c), device_id_type=MESH,
        )

    def pass_y(sh, g, h):
        block = grid_v.at[sh, g, me_y]
        return pltpu.make_async_remote_copy(
            src_ref=block, dst_ref=block, send_sem=y_send.at[sh, g, h], recv_sem=y_recv.at[sh, g, h],
            device_id=at(me_t, (y_up, y_down)[h], me_c), device_id_type=MESH,
        )

    def forward(sh, g, h):
        block = grid_v.at[sh, g, (y_down, y_up)[h], pl.ds(h * (HALF // 2), HALF // 2)]
        return pltpu.make_async_remote_copy(
            src_ref=block, dst_ref=block, send_sem=f_send.at[sh, g, h], recv_sem=f_recv.at[sh, g, h],
            device_id=at(me_t, (y_up, y_down)[h], me_c), device_id_type=MESH,
        )

    own_bunch = me_t // (n_theta // BUNCHES)

    def gather(sh, g):
        @pl.when(g == own_bunch)
        def _():
            arrived(sh, g, bunch - 1).wait_recv()

        @pl.when(g != own_bunch)
        def _():
            arrived(sh, g, bunch).wait_recv()

        spread[:bunch * span, :] = landed[sh, pl.ds(g * bunch, bunch)].astype(jnp.float32).reshape(bunch * span, 128)
        for r in range(HALF):
            grid_v[sh, g, me_y, r] = jnp.concatenate(
                [spread[pl.ds(r * 4 + p, bunch, stride=span), :] for p in range(4)], axis=0
            ).astype(jnp.bfloat16)
        pass_y(sh, g, 0).start()
        pass_y(sh, g, 1).start()

    def relay(sh, g):
        for h in range(2):
            pass_y(sh, g, h).wait_recv()
            forward(sh, g, h).start()

    def far(sh, g):
        for h in range(2):
            forward(sh, g, h).wait_recv()

    lax.fori_loop(0, 2 * tiles, stage, 0)
    send_half(0)
    lax.fori_loop(2, slots, mask_sky, 0)
    lax.fori_loop(2 * tiles, 4 * tiles, stage, 0)
    gather(0, 0)
    send_half(1)

    for r in reads[2:]:
        r.wait()
    index_v[0] = (cells_v[1] * QP + cells_v[0]) * 4
    index_v[1] = cells_v[2]
    to_smem = [pltpu.make_async_copy(index_v.at[n], dst, idx_sem.at[n]) for n, dst in enumerate((base_s, orient_s))]
    for copy in to_smem:
        copy.start()

    def product(sh, bunches, pair):
        count = bunches.stop - bunches.start
        right = jnp.concatenate(
            [grid_v[sh, bunches, :, 2 * pair + h].reshape(count * wide, 128) for h in range(2)], axis=1
        )
        left = table_v[sh, :, bunches.start * wide:bunches.stop * wide]
        return jnp.dot(left, right, preferred_element_type=jnp.float32)

    def first_part(pair, _):
        part_v[pair] = product(0, slice(0, BUNCHES), pair)
        return 0

    def second_part(pair, _):
        part_v[pair] += product(1, slice(0, BUNCHES - 1), pair)
        return 0

    def step(n, _):
        @pl.when(n == BUNCHES)
        def _():
            lax.fori_loop(0, 2 * BUNCHES, table, 0)

        @pl.when(n < 2 * BUNCHES)
        def _():
            gather(n // BUNCHES, n % BUNCHES)

        @pl.when(n >= LAG)
        def _():
            relay((n - LAG) // BUNCHES, (n - LAG) % BUNCHES)

        return 0

    lax.fori_loop(1, 2 * BUNCHES + LAG, step, 0)
    for g in range(BUNCHES):
        far(0, g)
    lax.fori_loop(0, pairs, first_part, 0)
    for g in range(BUNCHES - 1):
        far(1, g)
    lax.fori_loop(0, pairs, second_part, 0)

    def share(n):
        return pltpu.make_async_remote_copy(
            src_ref=share_out.at[n], dst_ref=share_in.at[n], send_sem=s_send.at[n], recv_sem=s_recv.at[n],
            device_id=at(me_t, me_y, 1 - me_c), device_id_type=MESH,
        )

    def halo(n):
        t = (me_t + n_theta - 1 + 2 * me_c) % n_theta
        return pltpu.make_async_remote_copy(
            src_ref=halo_out.at[n], dst_ref=halo_in.at[1 - me_c], send_sem=h_send.at[n], recv_sem=h_recv.at[1 - me_c],
            device_id=at(t, me_y, (me_c + n) % 2), device_id_type=MESH,
        )

    edge_goes = jnp.logical_or(
        jnp.logical_and(me_c == 0, me_t > 0), jnp.logical_and(me_c == 1, me_t < n_theta - 1)
    )

    def put_taps(cell, b, value):
        for e, rows in enumerate((value, pltpu.roll(value, PSI - 1, 1))):
            taps[pl.ds(cell * (QP * 4) + 2 * b + e, QP, stride=4), :] = rows

    def put_cycle(r, value):
        turned = pltpu.roll(value, PSI - 1, 1)
        for cell, b in ((r + 1, 0), (r, 1)):
            for e, rows in enumerate((value, turned)):
                taps[pl.ds(cell * (QP * 4) + 2 * b + e, QP, stride=4), :] = rows

    def pair_at(n, c):
        return n + c * (pairs - 1 - 2 * n)

    def finish(n, _):
        pair = pair_at(n, me_c)

        both = product(1, slice(BUNCHES - 1, BUNCHES), pair) + part_v[pair]
        for h in range(2):
            share_out[n, h] = both[QP:, h * 128:(h + 1) * 128].astype(jnp.bfloat16)
        share(n).start()

        @pl.when(n == 0)
        def _():
            for i in range(2):
                rows = both[i * QP:(i + 1) * QP]
                halo_out[i] = jnp.where(me_c == 0, rows[:, :128], rows[:, 128:]).astype(jnp.bfloat16)

        @pl.when(jnp.logical_and(n == 0, edge_goes))
        def _():
            halo(0).start()
            halo(1).start()

        part_v[pair, :QP] = both[:QP]
        return 0

    def put_own(pair, _):
        for h in range(2):
            put_cycle(me_c * HALF + 2 * pair + h, part_v[pair, :QP, h * 128:(h + 1) * 128])
        return 0

    far(1, BUNCHES - 1)
    lax.fori_loop(0, pairs, finish, 0)
    lax.fori_loop(0, pairs, put_own, 0)

    def take_share(n, _):
        share(n).wait_recv()
        for h in range(2):
            put_cycle((1 - me_c) * HALF + 2 * pair_at(n, 1 - me_c) + h, share_in[n, h].astype(jnp.float32))
        return 0

    lax.fori_loop(0, pairs, take_share, 0)

    def edge_in(slot):
        return pltpu.make_async_remote_copy(
            src_ref=halo_out.at[0], dst_ref=halo_in.at[slot], send_sem=h_send.at[0], recv_sem=h_recv.at[slot],
            device_id=at(me_t, me_y, 1 - me_c), device_id_type=MESH,
        )

    for slot, at_end in ((0, me_t == 0), (1, me_t == n_theta - 1)):
        @pl.when(jnp.logical_not(at_end))
        def _():
            edge_in(slot).wait_recv()

        @pl.when(at_end)
        def _():
            halo_in[slot] = jnp.zeros((QP, 128), jnp.bfloat16)

        put_taps(slot * RT, slot, halo_in[slot].astype(jnp.float32))

    for copy in to_smem:
        copy.wait()
    lane = lax.broadcasted_iota(jnp.int32, (8, 128), 1)

    count = count_s[0]

    def group(g, _):
        picked = jnp.zeros((8, 128), jnp.float32)
        for n in range(128):
            eight = taps[pl.ds(base_s[g, n], 8), :]
            tap = jnp.sum(jnp.where(lane == orient_s[g, n], eight, 0.0), axis=1, keepdims=True)
            picked = jnp.where(lane == n, tap, picked)
        weights = weight_v[:, pl.ds(pl.multiple_of(g * 128, 128), 128)]
        value = jnp.sum(picked * weights, axis=0, keepdims=True)
        out_ref[pl.ds(g, 1), :] = jnp.where(lane[0:1, :] + g * 128 < count, value, 0.0)
        return 0

    lax.fori_loop(0, groups, group, 0)

    @pl.when(edge_goes)
    def _():
        halo(0).wait_send()
        halo(1).wait_send()

    def drain(sh, _):
        arrived(sh, 0, others).wait_send()
        for g in range(BUNCHES):
            for h in range(2):
                pass_y(sh, g, h).wait_send()
                forward(sh, g, h).wait_send()
        return 0

    lax.fori_loop(0, 2, drain, 0)

    def drain_share(n, _):
        share(n).wait_send()
        return 0

    lax.fori_loop(0, pairs, drain_share, 0)


def shards(
    alm, wig, slot_order, beam, phi_cell, theta_cell, orient_cell_index, tap_weight, sample_count
):
    n_theta, n_phi = lax.axis_size("theta"), lax.axis_size("phi")
    slots, _, ldeg = alm.shape
    m_all = slot_order.shape[0]
    tile = min(ldeg // 2, 4096)
    tiles = ldeg // tile
    n_y = n_phi // 2
    sources = 2 * n_theta
    block = 4 * sources // BUNCHES
    pairs = HALF // 2
    groups = phi_cell.shape[0] // 128
    cells = [c.reshape(groups, 128) for c in (phi_cell, theta_cell, orient_cell_index)]
    anywhere = pl.BlockSpec(memory_space=pl.ANY)
    dma = pltpu.SemaphoreType.DMA
    f32, bf16, i32 = jnp.float32, jnp.bfloat16, jnp.int32
    value = pl.pallas_call(
        functools.partial(kernel, n_theta, n_phi, slots, ldeg, tile, m_all, groups),
        out_shape=jax.ShapeDtypeStruct((groups, 128), f32),
        in_specs=[anywhere] * 9,
        out_specs=pl.BlockSpec(memory_space=pltpu.VMEM),
        scratch_shapes=[
            pltpu.VMEM((slots * tiles, wig.shape[1], tile), bf16),
            pltpu.VMEM(beam.shape, bf16),
            pltpu.VMEM((tiles, 128, tile), bf16),
            pltpu.VMEM(alm.shape, bf16),
            pltpu.VMEM((slots, 2, 16, ldeg), bf16),
            pltpu.VMEM((1, m_all), i32),
            pltpu.VMEM((3, groups, 128), i32),
            pltpu.VMEM(tap_weight.shape, f32),
            pltpu.VMEM((256, 256), bf16),
            pltpu.VMEM((2, n_theta * RT, 256), f32),
            pltpu.VMEM((n_theta * RT * 4 + 8, 128), f32),
            pltpu.VMEM((2, n_theta * RT * 4, 128), bf16),
            pltpu.VMEM((2, sources, HALF * 4, 128), bf16),
            pltpu.VMEM((sources // BUNCHES * HALF * 4 + HALF * 4, 128), f32),
            pltpu.VMEM((2, BUNCHES, n_y, HALF, block, 128), bf16),
            pltpu.VMEM((2, 2 * QP, BUNCHES * n_y * block), bf16),
            pltpu.VMEM((pairs, 2 * QP, 256), f32),
            pltpu.VMEM((pairs, 2, QP, 128), bf16),
            pltpu.VMEM((pairs, 2, QP, 128), bf16),
            pltpu.VMEM((2, QP, 128), bf16),
            pltpu.VMEM((2, QP, 128), bf16),
            pltpu.VMEM(((RT + 1) * QP * 4 + 8, 128), f32),
            pltpu.VMEM((2, groups, 128), i32),
            pltpu.SMEM((groups, 128), i32),
            pltpu.SMEM((groups, 128), i32),
            pltpu.SMEM((1,), i32),
            dma((slots * tiles,)), dma((tiles,)), dma((7,)), dma((2,)),
            dma((2,)), dma((2, BUNCHES)),
            dma((2, BUNCHES, 2)), dma((2, BUNCHES, 2)),
            dma((2, BUNCHES, 2)), dma((2, BUNCHES, 2)),
            dma((pairs,)), dma((pairs,)),
            dma((2,)), dma((2,)),
        ],
        compiler_params=pltpu.CompilerParams(
            collective_id=0, has_side_effects=True, vmem_limit_bytes=58 << 20
        ),
        name="convolve",
    )(wig, alm, beam, slot_order.reshape(1, -1), *cells, tap_weight, sample_count)
    return value.reshape(-1)


def solution(mesh):
    return jax.shard_map(
        shards,
        mesh=mesh,
        in_specs=(
            P(("theta", "phi"), None, None),
            P(("theta", "phi"), None, None),
            P(),
            P(),
            P(("theta", "phi")),
            P(("theta", "phi")),
            P(("theta", "phi")),
            P(None, ("theta", "phi")),
            P(("theta", "phi")),
        ),
        out_specs=P(("theta", "phi")),
        check_vma=False,
    )
```

```python
import functools
import math

import jax
import jax.numpy as jnp
from jax import lax
from jax.experimental import pallas as pl
from jax.experimental.pallas import tpu as pltpu
from jax.sharding import PartitionSpec as P

PSI = 128
PD = 192
RT = 16
QP = 208
HALF = RT // 2
BUNCHES = 2
LAG = 3
MESH = pl.DeviceIdType.MESH
NT = (((1,), (1,)), ((), ()))


def slot_m(order, half, m_all):
    stride = max(half // m_all, 1)
    m = lax.shift_right_logical(order * half, m_all.bit_length() - 1)
    if stride > 1:
        m = m + (7 * order) % stride
    return m


def turn_cos(phase, total):
    x = (jnp.abs(phase - total / 2) - total / 4) * (2.0 * math.pi / total)
    x2 = x * x
    p = jnp.float32(-1.0 / math.factorial(11))
    for n in (9, 7, 5, 3, 1):
        p = p * x2 + jnp.float32((-1) ** (n // 2) / math.factorial(n))
    return p * x


def wrap(value, total):
    return value - jnp.floor((value + 0.5) * jnp.float32(1.0 / total)) * total


def psi_rows():
    k_at = lax.broadcasted_iota(jnp.int32, (128, 128), 0)
    p_at = lax.broadcasted_iota(jnp.int32, (128, 128), 1)
    turn = ((k_at * p_at) & (PSI - 1)).astype(jnp.float32)
    scale = 1.0 / math.sqrt(2 * 128)
    psi0 = turn_cos(turn, PSI) * scale
    psi1 = -turn_cos(wrap(turn + 0.75 * PSI, PSI), PSI) * scale
    return psi0.astype(jnp.bfloat16), psi1.astype(jnp.bfloat16), (-psi0).astype(jnp.bfloat16)


def kernel(
    n_theta, n_phi, slots, ldeg, tile, m_all, groups,
    wig_hbm, alm_hbm, beam_hbm, order_hbm, phi_hbm, theta_hbm, orient_hbm, weight_hbm, count_hbm, out_ref,
    wig_v, beam_v, beam_t, alm_v, sky_v, order_v, cells_v, weight_v, psi_v, sums, x32, x16, landed, spread, grid_v,
    table_v, part_v, share_out, share_in, halo_out, halo_in, taps, index_v,
    base_s, orient_s, count_s, wig_sem, beam_sem, in_sem, idx_sem, a_send, a_recv, y_send, y_recv, f_send, f_recv, s_send, s_recv, h_send, h_recv,
):
    me_t = lax.axis_index("theta")
    me_p = lax.axis_index("phi")
    me_y, me_c = me_p // 2, me_p % 2
    n_y = n_phi // 2
    total = PD * n_phi
    tiles = ldeg // tile
    sources = 2 * n_theta
    bunch = sources // BUNCHES
    span = HALF * 4
    per_block = 4 * bunch
    wide = n_y * per_block
    pairs = HALF // 2
    y_up, y_down, y_far = (me_y + 1) % n_y, (me_y + n_y - 1) % n_y, (me_y + 2) % n_y

    def at(t, y, c):
        return (t, y * 2 + c)

    reads = [
        pltpu.make_async_copy(src, dst, in_sem.at[n])
        for n, (src, dst) in enumerate(
            (
                (alm_hbm, alm_v), (order_hbm, order_v), (count_hbm, count_s), (phi_hbm, cells_v.at[0]),
                (theta_hbm, cells_v.at[1]), (orient_hbm, cells_v.at[2]), (weight_hbm, weight_v),
            )
        )
    ]

    def place(n):
        sh, i, s2 = n // (2 * tiles), n // 2 % tiles, n % 2
        return sh * 2 + s2, i

    def wig_copy(n):
        s, i = place(n)
        return pltpu.make_async_copy(
            wig_hbm.at[s, :, pl.ds(pl.multiple_of(i * tile, 128), tile)], wig_v.at[n], wig_sem.at[n]
        )

    def beam_copy(i):
        part = pl.ds(pl.multiple_of(i * tile, 128), tile)
        return pltpu.make_async_copy(beam_hbm.at[part, :], beam_v.at[part, :], beam_sem.at[i])

    for r in reads[:2]:
        r.start()
    for i in range(tiles):
        beam_copy(i).start()

    def wig_start(n, _):
        wig_copy(n).start()
        return 0

    lax.fori_loop(0, 2 * tiles, wig_start, 0)
    for r in reads[2:]:
        r.start()

    def target(n):
        m = n + 5 * sources // 8
        return (me_t + m // 2) & (n_theta - 1), (me_c + m) & 1

    barrier = pltpu.get_barrier_semaphore()

    def greet(n, _):
        t, c = target(n)

        @pl.when(n != alone)
        def _():
            pl.semaphore_signal(barrier, inc=1, device_id=at(t, me_y, c), device_id_type=MESH)

        return 0

    others = sources - 1
    alone = sources - 5 * sources // 8
    lax.fori_loop(0, sources, greet, 0)
    for y in (y_up, y_down):
        pl.semaphore_signal(barrier, inc=1, device_id=at(me_t, y, me_c), device_id_type=MESH)

    psi0, psi1, psi2 = psi_rows()
    psi_v[:128, :128] = psi0
    psi_v[:128, 128:] = psi1
    psi_v[128:, :128] = psi1
    psi_v[128:, 128:] = psi2
    for r in reads[:2]:
        r.wait()

    m_row = slot_m(order_v[...], total // 2, m_all)
    slot_lane = lax.broadcasted_iota(jnp.int32, (1, m_all), 1)
    eye = (
        lax.broadcasted_iota(jnp.int32, (128, 128), 0) == lax.broadcasted_iota(jnp.int32, (128, 128), 1)
    ).astype(jnp.bfloat16)

    m_hi = lax.shift_right_logical(m_row, 4).astype(jnp.float32)
    m_lo = (m_row & 15).astype(jnp.float32)
    split = jnp.concatenate([m_hi, m_lo, jnp.zeros((6, m_all), jnp.float32)], axis=0).astype(jnp.bfloat16)
    col = lax.broadcasted_iota(jnp.int32, (1, wide), 1)
    part = col % per_block // bunch
    source = col % bunch
    slot_col = (source // 2 * n_phi + col // per_block * 2 + source % 2) * slots + part // 2
    n_at = lax.broadcasted_iota(jnp.int32, (m_all, wide), 0)
    part_at = (part % 2).astype(jnp.float32)
    row = lax.broadcasted_iota(jnp.int32, (2 * QP, 1), 0)
    sibling = me_y * 2 + 1 - me_c
    q_at = jnp.where(row < QP, row + me_p * PD, row - QP + sibling * PD) - 1 + total
    q_at = q_at.astype(jnp.float32)

    def table(n, _):
        sh, g = n // BUNCHES, n % BUNCHES
        first = g * (n_theta // BUNCHES) * n_phi * slots + sh * 2
        pick = (n_at == slot_col + first).astype(jnp.bfloat16)
        moved = jnp.dot(split, pick, preferred_element_type=jnp.float32)
        m_col = moved[0:1, :] * 16.0 + moved[1:2, :]
        phase = wrap(m_col * q_at + (1.0 - part_at * 0.25) * total, total)
        table_v[sh, :, pl.ds(pl.multiple_of(g * wide, wide), wide)] = (
            turn_cos(phase, total) * (1.0 / math.sqrt(m_all))
        ).astype(jnp.bfloat16)
        return 0

    def turn_beam(i, _):
        beam_copy(i).wait()
        beam_t[i] = lax.dot_general(
            eye, beam_v[pl.ds(pl.multiple_of(i * tile, 128), tile), :], NT, preferred_element_type=jnp.float32
        ).astype(jnp.bfloat16)
        return 0

    def mask_sky(s, _):
        mine = slot_lane == (me_t * n_phi + me_p) * slots + s
        m_own = jnp.sum(jnp.where(mine, m_row, 0).astype(jnp.float32), axis=1, keepdims=True)
        degree = lax.broadcasted_iota(jnp.int32, (2, ldeg), 1).astype(jnp.float32)
        sky = jnp.where(degree >= m_own, alm_v[s].astype(jnp.float32), 0.0)
        for c in range(2):
            sky_v[s, c] = jnp.broadcast_to(sky[c:c + 1, :], (16, ldeg)).astype(jnp.bfloat16)
        return 0

    lax.fori_loop(0, 2, mask_sky, 0)
    lax.fori_loop(0, tiles, turn_beam, 0)

    def stage(n, _):
        s, i = place(n)
        part = beam_t[i].reshape(8, 16, tile)
        span_i = pl.ds(pl.multiple_of(i * tile, 128), tile)
        weighted = jnp.concatenate(
            [(part * sky_v[s, c, :, span_i][None]).reshape(128, tile) for c in range(2)], axis=0
        )
        wig_copy(n).wait()

        @pl.when(n < (slots - 2) * tiles)
        def _():
            wig_copy(n + 2 * tiles).start()

        term = lax.dot_general(wig_v[n], weighted, NT, preferred_element_type=jnp.float32)

        @pl.when(i == 0)
        def _():
            sums[n % 2] = term

        @pl.when(i > 0)
        def _():
            sums[n % 2] += term

        return 0

    def rows_of(t, c):
        return pl.ds(pl.multiple_of((t * 2 + c) * span, 16), span)

    def send_half(sh):
        def to_psi(s2, _):
            x = jnp.dot(sums[s2].astype(jnp.bfloat16), psi_v[...], preferred_element_type=jnp.float32)
            for c in range(2):
                x32[pl.ds(2 * s2 + c, n_theta * RT, stride=4), :] = x[:, c * 128:(c + 1) * 128]
            return 0

        lax.fori_loop(0, 2, to_psi, 0)

        x16[sh] = x32[:n_theta * RT * 4, :].astype(jnp.bfloat16)

        if sh == 0:
            pl.semaphore_wait(barrier, others + 2)

        def send(n, _):
            t, c = target(n)

            @pl.when(n != alone)
            def _():
                pltpu.make_async_remote_copy(
                    src_ref=x16.at[sh, rows_of(t, c), :], dst_ref=landed.at[sh, me_t * 2 + me_c],
                    send_sem=a_send.at[sh], recv_sem=a_recv.at[sh, me_t // (n_theta // BUNCHES)],
                    device_id=at(t, me_y, c), device_id_type=MESH,
                ).start()

            return 0

        lax.fori_loop(0, sources, send, 0)
        landed[sh, me_t * 2 + me_c] = x16[sh, rows_of(me_t, me_c), :]

    def arrived(sh, g, count):
        block = landed.at[sh, pl.ds(0, count)]
        return pltpu.make_async_remote_copy(
            src_ref=block, dst_ref=block, send_sem=a_send.at[sh], recv_sem=a_recv.at[sh, g],
            device_id=at(me_t, me_y, 1 - me_c), device_id_type=MESH,
        )

    def pass_y(sh, g, h):
        block = grid_v.at[sh, g, me_y]
        return pltpu.make_async_remote_copy(
            src_ref=block, dst_ref=block, send_sem=y_send.at[sh, g, h], recv_sem=y_recv.at[sh, g, h],
            device_id=at(me_t, (y_up, y_down)[h], me_c), device_id_type=MESH,
        )

    def forward(sh, g, h):
        block = grid_v.at[sh, g, (y_down, y_up)[h], pl.ds(h * (HALF // 2), HALF // 2)]
        return pltpu.make_async_remote_copy(
            src_ref=block, dst_ref=block, send_sem=f_send.at[sh, g, h], recv_sem=f_recv.at[sh, g, h],
            device_id=at(me_t, (y_up, y_down)[h], me_c), device_id_type=MESH,
        )

    own_bunch = me_t // (n_theta // BUNCHES)

    def gather(sh, g):
        @pl.when(g == own_bunch)
        def _():
            arrived(sh, g, bunch - 1).wait_recv()

        @pl.when(g != own_bunch)
        def _():
            arrived(sh, g, bunch).wait_recv()

        spread[:bunch * span, :] = landed[sh, pl.ds(g * bunch, bunch)].astype(jnp.float32).reshape(bunch * span, 128)
        for r in range(HALF):
            grid_v[sh, g, me_y, r] = jnp.concatenate(
                [spread[pl.ds(r * 4 + p, bunch, stride=span), :] for p in range(4)], axis=0
            ).astype(jnp.bfloat16)
        pass_y(sh, g, 0).start()
        pass_y(sh, g, 1).start()

    def relay(sh, g):
        for h in range(2):
            pass_y(sh, g, h).wait_recv()
            forward(sh, g, h).start()

    def far(sh, g):
        for h in range(2):
            forward(sh, g, h).wait_recv()

    lax.fori_loop(0, 2 * tiles, stage, 0)
    send_half(0)
    lax.fori_loop(2, slots, mask_sky, 0)
    lax.fori_loop(2 * tiles, 4 * tiles, stage, 0)
    gather(0, 0)
    send_half(1)

    for r in reads[2:]:
        r.wait()
    index_v[0] = (cells_v[1] * QP + cells_v[0]) * 4
    index_v[1] = cells_v[2]
    to_smem = [pltpu.make_async_copy(index_v.at[n], dst, idx_sem.at[n]) for n, dst in enumerate((base_s, orient_s))]
    for copy in to_smem:
        copy.start()

    def product(sh, bunches, pair):
        count = bunches.stop - bunches.start
        right = jnp.concatenate(
            [grid_v[sh, bunches, :, 2 * pair + h].reshape(count * wide, 128) for h in range(2)], axis=1
        )
        left = table_v[sh, :, bunches.start * wide:bunches.stop * wide]
        return jnp.dot(left, right, preferred_element_type=jnp.float32)

    def first_part(pair, _):
        part_v[pair] = product(0, slice(0, BUNCHES), pair)
        return 0

    def second_part(pair, _):
        part_v[pair] += product(1, slice(0, BUNCHES - 1), pair)
        return 0

    def step(n, _):
        @pl.when(n == BUNCHES)
        def _():
            lax.fori_loop(0, 2 * BUNCHES, table, 0)

        @pl.when(n < 2 * BUNCHES)
        def _():
            gather(n // BUNCHES, n % BUNCHES)

        @pl.when(n >= LAG)
        def _():
            relay((n - LAG) // BUNCHES, (n - LAG) % BUNCHES)

        return 0

    lax.fori_loop(1, 2 * BUNCHES + LAG, step, 0)
    for g in range(BUNCHES):
        far(0, g)
    lax.fori_loop(0, pairs, first_part, 0)
    for g in range(BUNCHES - 1):
        far(1, g)
    lax.fori_loop(0, pairs, second_part, 0)

    def share(n):
        return pltpu.make_async_remote_copy(
            src_ref=share_out.at[n], dst_ref=share_in.at[n], send_sem=s_send.at[n], recv_sem=s_recv.at[n],
            device_id=at(me_t, me_y, 1 - me_c), device_id_type=MESH,
        )

    def halo(n):
        t = (me_t + n_theta - 1 + 2 * me_c) % n_theta
        return pltpu.make_async_remote_copy(
            src_ref=halo_out.at[n], dst_ref=halo_in.at[1 - me_c], send_sem=h_send.at[n], recv_sem=h_recv.at[1 - me_c],
            device_id=at(t, me_y, (me_c + n) % 2), device_id_type=MESH,
        )

    edge_goes = jnp.logical_or(
        jnp.logical_and(me_c == 0, me_t > 0), jnp.logical_and(me_c == 1, me_t < n_theta - 1)
    )

    def put_taps(cell, b, value):
        for e, rows in enumerate((value, pltpu.roll(value, PSI - 1, 1))):
            taps[pl.ds(cell * (QP * 4) + 2 * b + e, QP, stride=4), :] = rows

    def put_cycle(r, value):
        turned = pltpu.roll(value, PSI - 1, 1)
        for cell, b in ((r + 1, 0), (r, 1)):
            for e, rows in enumerate((value, turned)):
                taps[pl.ds(cell * (QP * 4) + 2 * b + e, QP, stride=4), :] = rows

    def pair_at(n, c):
        return n + c * (pairs - 1 - 2 * n)

    def finish(n, _):
        pair = pair_at(n, me_c)

        both = product(1, slice(BUNCHES - 1, BUNCHES), pair) + part_v[pair]
        for h in range(2):
            share_out[n, h] = both[QP:, h * 128:(h + 1) * 128].astype(jnp.bfloat16)
        share(n).start()

        @pl.when(n == 0)
        def _():
            for i in range(2):
                rows = both[i * QP:(i + 1) * QP]
                halo_out[i] = jnp.where(me_c == 0, rows[:, :128], rows[:, 128:]).astype(jnp.bfloat16)

        @pl.when(jnp.logical_and(n == 0, edge_goes))
        def _():
            halo(0).start()
            halo(1).start()

        part_v[pair, :QP] = both[:QP]
        return 0

    def put_own(pair, _):
        for h in range(2):
            put_cycle(me_c * HALF + 2 * pair + h, part_v[pair, :QP, h * 128:(h + 1) * 128])
        return 0

    far(1, BUNCHES - 1)
    lax.fori_loop(0, pairs, finish, 0)
    lax.fori_loop(0, pairs, put_own, 0)

    def take_share(n, _):
        share(n).wait_recv()
        for h in range(2):
            put_cycle((1 - me_c) * HALF + 2 * pair_at(n, 1 - me_c) + h, share_in[n, h].astype(jnp.float32))
        return 0

    lax.fori_loop(0, pairs, take_share, 0)

    def edge_in(slot):
        return pltpu.make_async_remote_copy(
            src_ref=halo_out.at[0], dst_ref=halo_in.at[slot], send_sem=h_send.at[0], recv_sem=h_recv.at[slot],
            device_id=at(me_t, me_y, 1 - me_c), device_id_type=MESH,
        )

    for slot, at_end in ((0, me_t == 0), (1, me_t == n_theta - 1)):
        @pl.when(jnp.logical_not(at_end))
        def _():
            edge_in(slot).wait_recv()

        @pl.when(at_end)
        def _():
            halo_in[slot] = jnp.zeros((QP, 128), jnp.bfloat16)

        put_taps(slot * RT, slot, halo_in[slot].astype(jnp.float32))

    for copy in to_smem:
        copy.wait()
    lane = lax.broadcasted_iota(jnp.int32, (8, 128), 1)

    count = count_s[0]

    def group(g):
        picked = jnp.zeros((8, 128), jnp.float32)
        for n in range(128):
            eight = taps[pl.ds(base_s[g, n], 8), :]
            tap = jnp.sum(jnp.where(lane == orient_s[g, n], eight, 0.0), axis=1, keepdims=True)
            picked = jnp.where(lane == n, tap, picked)
        weights = weight_v[:, pl.ds(pl.multiple_of(g * 128, 128), 128)]
        value = jnp.sum(picked * weights, axis=0, keepdims=True)
        out_ref[pl.ds(g, 1), :] = jnp.where(lane[0:1, :] + g * 128 < count, value, 0.0)

    def some_groups(n, _):
        for k in range(4):
            group(4 * n + k)
        return 0

    lax.fori_loop(0, groups // 4, some_groups, 0)

    @pl.when(edge_goes)
    def _():
        halo(0).wait_send()
        halo(1).wait_send()

    def drain(sh, _):
        arrived(sh, 0, others).wait_send()
        for g in range(BUNCHES):
            for h in range(2):
                pass_y(sh, g, h).wait_send()
                forward(sh, g, h).wait_send()
        return 0

    lax.fori_loop(0, 2, drain, 0)

    def drain_share(n, _):
        share(n).wait_send()
        return 0

    lax.fori_loop(0, pairs, drain_share, 0)


def shards(
    alm, wig, slot_order, beam, phi_cell, theta_cell, orient_cell_index, tap_weight, sample_count
):
    n_theta, n_phi = lax.axis_size("theta"), lax.axis_size("phi")
    slots, _, ldeg = alm.shape
    m_all = slot_order.shape[0]
    tile = min(ldeg // 2, 4096)
    tiles = ldeg // tile
    n_y = n_phi // 2
    sources = 2 * n_theta
    block = 4 * sources // BUNCHES
    pairs = HALF // 2
    groups = phi_cell.shape[0] // 128
    cells = [c.reshape(groups, 128) for c in (phi_cell, theta_cell, orient_cell_index)]
    anywhere = pl.BlockSpec(memory_space=pl.ANY)
    dma = pltpu.SemaphoreType.DMA
    f32, bf16, i32 = jnp.float32, jnp.bfloat16, jnp.int32
    value = pl.pallas_call(
        functools.partial(kernel, n_theta, n_phi, slots, ldeg, tile, m_all, groups),
        out_shape=jax.ShapeDtypeStruct((groups, 128), f32),
        in_specs=[anywhere] * 9,
        out_specs=pl.BlockSpec(memory_space=pltpu.VMEM),
        scratch_shapes=[
            pltpu.VMEM((slots * tiles, wig.shape[1], tile), bf16),
            pltpu.VMEM(beam.shape, bf16),
            pltpu.VMEM((tiles, 128, tile), bf16),
            pltpu.VMEM(alm.shape, bf16),
            pltpu.VMEM((slots, 2, 16, ldeg), bf16),
            pltpu.VMEM((1, m_all), i32),
            pltpu.VMEM((3, groups, 128), i32),
            pltpu.VMEM(tap_weight.shape, f32),
            pltpu.VMEM((256, 256), bf16),
            pltpu.VMEM((2, n_theta * RT, 256), f32),
            pltpu.VMEM((n_theta * RT * 4 + 8, 128), f32),
            pltpu.VMEM((2, n_theta * RT * 4, 128), bf16),
            pltpu.VMEM((2, sources, HALF * 4, 128), bf16),
            pltpu.VMEM((sources // BUNCHES * HALF * 4 + HALF * 4, 128), f32),
            pltpu.VMEM((2, BUNCHES, n_y, HALF, block, 128), bf16),
            pltpu.VMEM((2, 2 * QP, BUNCHES * n_y * block), bf16),
            pltpu.VMEM((pairs, 2 * QP, 256), f32),
            pltpu.VMEM((pairs, 2, QP, 128), bf16),
            pltpu.VMEM((pairs, 2, QP, 128), bf16),
            pltpu.VMEM((2, QP, 128), bf16),
            pltpu.VMEM((2, QP, 128), bf16),
            pltpu.VMEM(((RT + 1) * QP * 4 + 8, 128), f32),
            pltpu.VMEM((2, groups, 128), i32),
            pltpu.SMEM((groups, 128), i32),
            pltpu.SMEM((groups, 128), i32),
            pltpu.SMEM((1,), i32),
            dma((slots * tiles,)), dma((tiles,)), dma((7,)), dma((2,)),
            dma((2,)), dma((2, BUNCHES)),
            dma((2, BUNCHES, 2)), dma((2, BUNCHES, 2)),
            dma((2, BUNCHES, 2)), dma((2, BUNCHES, 2)),
            dma((pairs,)), dma((pairs,)),
            dma((2,)), dma((2,)),
        ],
        compiler_params=pltpu.CompilerParams(
            collective_id=0, has_side_effects=True, vmem_limit_bytes=58 << 20
        ),
        name="convolve",
    )(wig, alm, beam, slot_order.reshape(1, -1), *cells, tap_weight, sample_count)
    return value.reshape(-1)


def solution(mesh):
    return jax.shard_map(
        shards,
        mesh=mesh,
        in_specs=(
            P(("theta", "phi"), None, None),
            P(("theta", "phi"), None, None),
            P(),
            P(),
            P(("theta", "phi")),
            P(("theta", "phi")),
            P(("theta", "phi")),
            P(None, ("theta", "phi")),
            P(("theta", "phi")),
        ),
        out_specs=P(("theta", "phi")),
        check_vma=False,
    )
```
